32 devices in a mesh: dp: 4 (over x, core), seq: 8 (over z, y).
Axes of the slice: x: 2, y: 2, z: 4, core: 2. Of those that a mesh axis runs over, the one named last changes fastest.
Arguments:
- hidden: bfloat16 [4, 1024, 2048], P('dp', 'seq'), may hold values from -6 to 6
- tokens: int32 [4, 1024], P('dp', 'seq'), may hold values from 0 to 4
- embedding: float32 [5, 2048], replicated, may hold values from -6 to 6
- weight: bfloat16 [2048, 1024], P('dp'), may hold values from -0.125 to 0.125
- kernel: float32 [7, 1024], replicated, may hold values from -2.4 to 2.4
- cotangent: bfloat16 [4, 1024, 1024], P('dp', 'seq'), may hold values from -6 to 6
Outputs:
- block_result: bfloat16 [4, 1024, 1024], P('dp', 'seq')
- grad_hidden: bfloat16 [4, 1024, 2048], P('dp', 'seq')
- grad_weight: float32 [2048, 1024], P('dp')
- grad_kernel: float32 [7, 1024], replicated
- grad_embedding: float32 [5, 2048], replicated
The draws below stay inside these ranges and needn't reach their ends.
All inputs are finite; a program needn't handle non-finite values.
Results may differ from the reference program's by a relative error of at most 0.0095.
Values may be sent and summed in bfloat16 or wider, within the bound.
A program may use at most 64 MiB of HBM per device.

```python
import math
import jax
import jax.numpy as jnp
from jax import lax

D = 2048
UNITS = 1024
VOCAB = 5
REACH = 3
TAPS = 7
LENGTH = 1024
BATCH = 4


def place_ends(drawn, rng, smallest, high):
    dims = drawn.shape
    place = [jax.random.randint(jax.random.fold_in(rng, axis), (), 0, dims[axis]) for axis in range(len(dims))]
    drawn = drawn.at[tuple(place)].set(smallest)
    longest = dims.index(max(dims))
    place[longest] = (place[longest] + 1) % dims[longest]
    return drawn.at[tuple(place)].set(high)


def raised(array, own_key, source, target, shards_of, factor):
    owner, partner = [(jnp.arange(array.shape[axis_at]) // (array.shape[axis_at] // shards_of)).reshape([-1 if axis == axis_at else 1 for axis in range(array.ndim)]) for axis_at in (source, target)]
    chosen = jax.random.permutation(own_key, shards_of)[partner]
    strong = (owner == chosen) | (owner == (partner + shards_of // 2) % shards_of)
    return jnp.where(strong, factor * array, array)


def block_levels(stream_key, dims, split, least, largest):
    loudness = 1.0
    for position, shards_of in split:
        steps = jax.random.uniform(jax.random.fold_in(jax.random.fold_in(stream_key, 6), position), (shards_of,), jnp.float32, least / len(split), largest / len(split))
        loudness = loudness * jnp.repeat(jnp.exp(steps), dims[position] // shards_of).reshape((-1,) + (1,) * (len(dims) - 1 - position))
    return loudness


def normal_values(own_key, dims, deviation, reach, cuts=(), kind=jnp.bfloat16):
    entries = jax.random.normal(own_key, dims, jnp.float32) * deviation
    if len(cuts) > 0:
        entries = block_levels(own_key, dims, cuts, -0.22, 0.18) * entries
    return jnp.clip(entries, min=-reach, max=reach).astype(kind)


def noise_with(key, shape, spread, limit, shards, heavy, held_as=jnp.bfloat16):
    result = spread * jax.random.normal(key, shape, jnp.float32)
    if shards:
        result = result * block_levels(key, shape, shards, -0.22, 0.18)
    return jnp.clip(raised(result, jax.random.fold_in(key, 3), *heavy), -limit, limit).astype(held_as)


def setup_inputs(seed: int = 0) -> dict:
    seeds = jax.random.split(jax.random.key(seed), 7)
    return {
        "hidden": noise_with(seeds[0], (BATCH, LENGTH, D), 1.0, 6.0, ((0, 4), (1, 8)), (1, 2, 8, 2.0)),
        "tokens": place_ends(jax.random.randint(seeds[1], (BATCH, LENGTH), 0, VOCAB), jax.random.fold_in(seeds[1], 1), 0, VOCAB - 1).astype(jnp.int32),
        "embedding": normal_values(seeds[2], (VOCAB, D), 1.0, 6.0, (), jnp.float32),
        "weight": normal_values(seeds[3], (D, UNITS), D ** -0.5, 0.125, ((0, 4),)),
        "kernel": normal_values(seeds[4], (TAPS, UNITS), 0.4, 2.4, (), jnp.float32),
        "cotangent": normal_values(seeds[5], (BATCH, LENGTH, UNITS), 1.0, 6.0, ((0, 4), (1, 8))),
    }


def lookup(token_codes, embedding):
    running = jnp.zeros((token_codes.shape[0], embedding.shape[1]), jnp.float32)
    for symbol in range(embedding.shape[0]):
        running = running + jnp.where((token_codes == symbol)[:, None], embedding[symbol][None, :], 0.0)
    return running

def strand(inputs, upstream, weight, kernel):
    values = jnp.dot(inputs, weight, preferred_element_type=jnp.float32).astype(jnp.bfloat16)
    linear = values.astype(jnp.float32)
    widened = jnp.pad(linear, ((REACH, REACH), (0, 0)))
    mixing = kernel[0][None, :] * widened[0:LENGTH]
    for tap_index in range(1, TAPS):
        mixing = mixing + kernel[tap_index][None, :] * widened[tap_index:tap_index + LENGTH]
    logistic = jax.nn.sigmoid(linear)
    gating = linear * logistic
    strand_out = mixing * gating
    incoming = upstream.astype(jnp.float32)
    grad_mix = incoming * gating
    accumulated = incoming * mixing * logistic * (1.0 + linear * (1.0 - logistic))
    grad_padded = jnp.pad(grad_mix, ((REACH, REACH), (0, 0)))
    for tap_index in range(TAPS):
        lower = 2 * REACH - tap_index
        accumulated = accumulated + kernel[tap_index][None, :] * grad_padded[lower:lower + LENGTH]
    grad_values = accumulated.astype(jnp.bfloat16)
    kernel_grad = jnp.stack([lax.optimization_barrier(jnp.sum(grad_mix * widened[tap_index:tap_index + LENGTH], axis=0)) for tap_index in range(TAPS)])
    weight_grad = jnp.dot(inputs.T, grad_values, preferred_element_type=jnp.float32)
    returned = jnp.dot(grad_values, weight.T, preferred_element_type=jnp.float32)
    return (strand_out, kernel_grad, weight_grad, returned)

def one_window(window, token_codes, upstream, embedding, weight, kernel):
    stream = (window.astype(jnp.float32) + lookup(token_codes, embedding)).astype(jnp.bfloat16)
    reverse = stream[::-1, ::-1]
    out_fwd, kernel_fwd, weight_fwd, back_fwd = strand(stream, upstream, weight, kernel)
    out_rev, kernel_rev, weight_rev, back_rev = strand(reverse, upstream[::-1, ::-1], weight, kernel)
    rev_out = out_rev.astype(jnp.bfloat16)
    block_result = (out_fwd + rev_out.astype(jnp.float32)[::-1, ::-1]).astype(jnp.bfloat16)
    back_round = back_rev.astype(jnp.bfloat16)
    grad_stream = back_fwd + back_round.astype(jnp.float32)[::-1, ::-1]
    one_hot = (token_codes[:, None] == jnp.arange(VOCAB, dtype=jnp.int32)[None, :]).astype(jnp.float32)
    table_part = lax.dot_general(one_hot, grad_stream, (((0,), (0,)), ((), ())), precision=lax.Precision.HIGHEST, preferred_element_type=jnp.float32)
    return (block_result, grad_stream.astype(jnp.bfloat16), weight_fwd + weight_rev, kernel_fwd + kernel_rev, table_part)

def reference(hidden, tokens, embedding, weight, kernel, cotangent):
    block_result, grad_hidden, weight_all, kernel_all, table_all = lax.map(lambda pieces: one_window(pieces[0], pieces[1], pieces[2], embedding, weight, kernel), (hidden, tokens, cotangent))
    factor = 1.0 / math.sqrt(BATCH * LENGTH)
    return (block_result, grad_hidden, lax.optimization_barrier(jnp.sum(weight_all, axis=0)) * factor, lax.optimization_barrier(jnp.sum(kernel_all, axis=0)) * factor, lax.optimization_barrier(jnp.sum(table_all, axis=0)) * factor)
```

```python
import functools
import math

import jax
import jax.numpy as jnp
from jax import lax
from jax.experimental import pallas as pl
from jax.experimental.pallas import tpu as pltpu
from jax.sharding import PartitionSpec as P

MESH = pl.DeviceIdType.MESH
F32 = jnp.float32
BF16 = jnp.bfloat16
EDGE = 16
CHUNKS = 4
PIECES = 4
LANES = 256


def halvings(rows, bits):
    sizes = []
    for _ in range(bits):
        halved = rows // 2 >= 16 and rows % 32 == 0
        sizes.append((rows // 2 if halved else rows, halved))
        rows = sizes[-1][0]
    return sizes


def body(
    seq_count, bits,
    hid_ref, tokc_ref, tokr_ref, emb_ref, w_ref, ker_ref, cot_ref,
    block_ref, hout_ref, gw_ref, small_ref,
    wg, sx, hx, ux, hu, s2t, val, gmix, outs, routs, gv, fwd_back, rev_back,
    acc2, acc, core_send, core_recv, x_send, x_recv, seq_send, seq_recv,
    small, small_recv,
    w_ss, w_rs, h_ss, h_rs, r_ss, r_rs, s_ss, s_rs,
):
    rows = hid_ref.shape[0]
    depth, units = w_ref.shape
    width = hid_ref.shape[1]
    taps = ker_ref.shape[0]
    reach = (taps - 1) // 2
    vocab = emb_ref.shape[0]
    total = rows + 2 * EDGE
    dp = lax.axis_index("dp")
    seq = lax.axis_index("seq")
    xi, ci = dp // 2, dp % 2
    core_id = (dp + 1 - 2 * ci, seq)
    x_id = (dp + 2 - 4 * xi, seq)
    bit_vals = [(seq // (1 << b)) % 2 for b in range(bits)]
    bit_ids = [(dp, seq + (1 - 2 * bit_vals[b]) * (1 << b)) for b in range(bits)]
    left_id = (dp, (seq + seq_count - 1) % seq_count)
    right_id = (dp, (seq + 1) % seq_count)

    partners = [core_id, x_id] + bit_ids + [left_id, right_id]
    barrier = pltpu.get_barrier_semaphore()
    for partner in partners:
        pl.semaphore_signal(barrier, inc=1, device_id=partner, device_id_type=MESH)
    pl.semaphore_wait(barrier, len(partners))

    def remote(src, dst, ss, rs, who):
        return pltpu.make_async_remote_copy(
            src_ref=src, dst_ref=dst, send_sem=ss, recv_sem=rs, device_id=who, device_id_type=MESH
        )

    yi = bit_vals[0]
    y_id = bit_ids[0]
    dpx = dp + 2 - 4 * xi
    half = depth // 2
    piece = half // PIECES

    def span(side, p):
        return pl.ds(pl.multiple_of(side * half + p * piece, 16), piece)

    sends = []
    over_x = [
        remote(w_ref.at[span(yi, p)], wg.at[dp, span(yi, p)], w_ss.at[p], w_rs.at[p], x_id)
        for p in range(PIECES)
    ]
    for copy in over_x:
        copy.start()
    own = remote(w_ref, wg.at[dp], w_ss.at[4 * PIECES], w_rs.at[4 * PIECES], core_id)
    own.start()
    sends += over_x + [own]
    halo_u = [
        remote(cot_ref.at[pl.ds(rows - EDGE, EDGE)], hu.at[0], h_ss.at[0], h_rs.at[0], right_id),
        remote(cot_ref.at[pl.ds(0, EDGE)], hu.at[1], h_ss.at[1], h_rs.at[1], left_id),
    ]
    for copy in halo_u:
        copy.start()

    tile = LANES
    tok = tokc_ref[...]

    def stream_tile(i, carry):
        cols = pl.ds(pl.multiple_of(i * tile, tile), tile)
        looked = jnp.zeros((rows, tile), F32)
        for k in range(vocab):
            looked = looked + jnp.where(tok == k, emb_ref[pl.ds(k, 1), cols], 0.0)
        sx[0, pl.ds(EDGE, rows), cols] = (hid_ref[:, cols].astype(F32) + looked).astype(BF16)
        return carry

    lax.fori_loop(0, width // tile, stream_tile, 0)
    halo_s = [
        remote(sx.at[0, pl.ds(rows, EDGE)], hx.at[0], h_ss.at[2], h_rs.at[2], right_id),
        remote(sx.at[0, pl.ds(EDGE, EDGE)], hx.at[1], h_ss.at[3], h_rs.at[3], left_id),
    ]
    for copy in halo_s:
        copy.start()
    sends += halo_u + halo_s
    wg[dp] = w_ref[...]

    has_left = (seq > 0).astype(F32)
    has_right = (seq < seq_count - 1).astype(F32)
    ux[0, pl.ds(EDGE, rows), :] = cot_ref[...]
    for copy in halo_u + halo_s:
        copy.wait_recv()
    sx[0, pl.ds(0, EDGE), :] = (hx[0].astype(F32) * has_left).astype(BF16)
    sx[0, pl.ds(rows + EDGE, EDGE), :] = (hx[1].astype(F32) * has_right).astype(BF16)
    ux[0, pl.ds(0, EDGE), :] = (hu[0].astype(F32) * has_left).astype(BF16)
    ux[0, pl.ds(rows + EDGE, EDGE), :] = (hu[1].astype(F32) * has_right).astype(BF16)

    flip = (
        lax.broadcasted_iota(jnp.int32, (tile, tile), 0)
        + lax.broadcasted_iota(jnp.int32, (tile, tile), 1)
        == tile - 1
    ).astype(F32).astype(BF16)

    def mirrored(block):
        return jnp.dot(block, flip, preferred_element_type=F32)

    def reverse_stream(i, carry):
        cols = pl.ds(pl.multiple_of(i * tile, tile), tile)
        back = pl.ds(pl.multiple_of(width - tile - i * tile, tile), tile)
        sx[1, :, back] = mirrored(sx[0, :, cols]).astype(BF16)
        return carry

    lax.fori_loop(0, width // tile, reverse_stream, 0)

    def reverse_up(i, carry):
        cols = pl.ds(pl.multiple_of(i * tile, tile), tile)
        back = pl.ds(pl.multiple_of(units - tile - i * tile, tile), tile)
        ux[1, :, back] = mirrored(ux[0, :, cols]).astype(BF16)
        return carry

    lax.fori_loop(0, units // tile, reverse_up, 0)

    def project(block, first):
        depth_cols = pl.ds(pl.multiple_of(block * depth, depth), depth)

        def project_tile(i, carry):
            cols = pl.ds(pl.multiple_of(i * tile, tile), tile)
            for s in range(2):
                part = jnp.dot(sx[s, :, depth_cols], wg[block, :, cols], preferred_element_type=F32)
                if first:
                    val[s, :, cols] = part
                else:
                    val[s, :, cols] += part
            return carry

        lax.fori_loop(0, units // tile, project_tile, 0)

    project(dp, True)

    over_y, over_core = [], []
    for p in range(PIECES):
        over_x[p].wait_recv()
        over_y.append(
            remote(wg.at[dpx, span(yi, p)], wg.at[dpx, span(yi, p)], w_ss.at[PIECES + p], w_rs.at[PIECES + p], y_id)
        )
        over_core.append(
            remote(wg.at[dpx, span(yi, p)], wg.at[dpx, span(yi, p)], w_ss.at[2 * PIECES + p], w_rs.at[2 * PIECES + p], core_id)
        )
        over_y[p].start()
        over_core[p].start()
        if p == 0:
            own.wait_recv()
            project(dp + 1 - 2 * ci, False)

            def transpose_tile(i, carry):
                cols = pl.ds(pl.multiple_of(i * tile, tile), tile)
                for s in range(2):
                    s2t[cols, pl.ds(s * rows, rows)] = sx[s, pl.ds(EDGE, rows), cols].T
                return carry

            lax.fori_loop(0, width // tile, transpose_tile, 0)
    over_core2 = []
    for p in range(PIECES):
        over_y[p].wait_recv()
        other = 1 - yi
        over_core2.append(
            remote(wg.at[dpx, span(other, p)], wg.at[dpx, span(other, p)], w_ss.at[3 * PIECES + p], w_rs.at[3 * PIECES + p], core_id)
        )
        over_core2[p].start()
    sends += over_y + over_core + over_core2
    project(dpx, False)
    for p in range(PIECES):
        over_core[p].wait_recv()
        over_core2[p].wait_recv()
    project(dpx + 1 - 2 * ci, False)

    ew = 128
    lo = EDGE - 8

    def strand_tile(i, carry):
        cols = pl.ds(pl.multiple_of(i * ew, ew), ew)
        tap_sums = [jnp.zeros((1, ew), F32)] * taps
        for s in range(2):
            val[s, :, cols] = val[s, :, cols].astype(BF16).astype(F32)
            wide = val[s, pl.ds(lo, rows + 16), cols]
            gmix[s] = ux[s, :, cols].astype(F32)[lo : lo + rows + 16] * wide * jax.nn.sigmoid(wide)
            lin = val[s, pl.ds(EDGE, rows), cols]
            sig = jax.nn.sigmoid(lin)
            up = ux[s, pl.ds(EDGE, rows), cols].astype(F32)
            mine = gmix[s, pl.ds(8, rows), :]
            mixing = jnp.zeros((rows, ew), F32)
            spread = jnp.zeros((rows, ew), F32)
            for m in range(taps):
                k = m if s == 0 else taps - 1 - m
                row = ker_ref[pl.ds(k, 1), cols]
                shifted = val[s, pl.ds(EDGE + m - reach, rows), cols]
                mixing = mixing + row * shifted
                tap_sums[k] = tap_sums[k] + jnp.sum(mine * shifted, axis=0, keepdims=True)
                spread = spread + row * gmix[s, pl.ds(8 + reach - m, rows), :]
            gate = lin * sig
            strand_out = mixing * gate
            if s == 0:
                outs[:, cols] = strand_out
            else:
                routs[:, cols] = strand_out.astype(BF16)
            grad = up * mixing * sig * (1.0 + lin * (1.0 - sig)) + spread
            gv[pl.ds(s * rows, rows), cols] = grad.astype(BF16)
        small_cols = pl.ds(pl.multiple_of((i % (units // 2 // ew)) * ew, ew), ew)
        pad = [jnp.zeros((1, ew), F32)] * (8 - taps)
        small[i // (units // 2 // ew), pl.ds(0, 8), small_cols] = jnp.concatenate(tap_sums + pad, axis=0)
        return carry

    lax.fori_loop(0, units // ew, strand_tile, 0)

    cw = units // CHUNKS
    levels = halvings(depth, bits)

    def core_copy(j):
        return remote(core_send.at[j], core_recv.at[j], r_ss.at[j, 0], r_rs.at[j, 0], core_id)

    def x_copy(j):
        return remote(x_send.at[j], x_recv.at[j], r_ss.at[j, 1], r_rs.at[j, 1], x_id)

    def product(j):
        grads = gv[:, pl.ds(j * cw, cw)]

        def block_product(b, carry):
            theirs = pl.ds(pl.multiple_of((2 * b + 1 - ci) * depth, depth), depth)
            mine = pl.ds(pl.multiple_of((2 * b + ci) * depth, depth), depth)
            core_send[j, b] = jnp.dot(s2t[theirs, :], grads, preferred_element_type=F32).astype(BF16)
            acc2[j, b] = jnp.dot(s2t[mine, :], grads, preferred_element_type=F32)
            return carry

        lax.fori_loop(0, 2, block_product, 0)
        core_copy(j).start()

    def after_core(j):
        core_copy(j).wait_recv()
        x_send[j] = (acc2[j, 1 - xi] + core_recv[j, 1 - xi].astype(F32)).astype(BF16)
        x_copy(j).start()
        acc[j] = acc2[j, xi] + core_recv[j, xi].astype(F32)

    offsets = [0]
    starts = [0]
    off = 0
    spans_keep, spans_send = [], []
    for (size, halved), bit in zip(levels, bit_vals):
        if halved:
            keep, give = off + bit * size, off + (1 - bit) * size
        else:
            keep, give = off, off
        spans_keep.append(pl.ds(pl.multiple_of(keep, 16), size))
        spans_send.append(pl.ds(pl.multiple_of(give, 16), size))
        off = keep
    sub_at = []
    at = 0
    for size, _ in levels:
        sub_at.append(at)
        at += size

    def rs_copy(j, b):
        where = pl.ds(sub_at[b], levels[b][0])
        return remote(seq_send.at[j, where], seq_recv.at[j, where], r_ss.at[j, 2 + b], r_rs.at[j, 2 + b], bit_ids[b])

    def rs_start(j, b):
        seq_send[j, pl.ds(sub_at[b], levels[b][0]), :] = acc[j, spans_send[b], :].astype(BF16)
        rs_copy(j, b).start()

    def rs_finish(j, b):
        rs_copy(j, b).wait_recv()
        acc[j, spans_keep[b], :] += seq_recv[j, pl.ds(sub_at[b], levels[b][0]), :].astype(F32)

    gathers = [b for b in reversed(range(bits)) if levels[b][1]]

    def ag_copy(j, b):
        ref = gw_ref.at[j, spans_keep[b]]
        return remote(ref, ref, r_ss.at[j, 2 + bits + b], r_rs.at[j, 2 + bits + b], bit_ids[b])

    def stages(j):
        def after_x():
            x_copy(j).wait_recv()
            acc[j] += x_recv[j].astype(F32)
            rs_start(j, 0)

        def after_rs(b):
            rs_finish(j, b)
            if b + 1 < bits:
                rs_start(j, b + 1)
            else:
                gw_ref[j, spans_keep[-1], :] = acc[j, spans_keep[-1], :].astype(BF16)
                ag_copy(j, gathers[0]).start()

        def after_ag(n):
            ag_copy(j, gathers[n]).wait_recv()
            if n + 1 < len(gathers):
                ag_copy(j, gathers[n + 1]).start()

        steps = [after_x]
        steps += [functools.partial(after_rs, b) for b in range(bits)]
        steps += [functools.partial(after_ag, n) for n in range(len(gathers))]
        return steps

    for j in range(CHUNKS):
        product(j)
        if j > 0:
            after_core(j - 1)
    after_core(CHUNKS - 1)

    def back_tile(i, carry):
        b = i // (depth // tile)
        r = pl.ds(pl.multiple_of((i % (depth // tile)) * tile, tile), tile)
        cols = pl.ds(pl.multiple_of(i * tile, tile), tile)
        mirror = pl.ds(pl.multiple_of(width - tile - i * tile, tile), tile)
        part = lax.dot_general(gv[...], wg[b, r, :], (((1,), (1,)), ((), ())), preferred_element_type=F32)
        fwd_back[:, cols] = part[:rows]
        rev_back[:, mirror] = mirrored(part[rows:].astype(BF16))
        return carry

    lax.fori_loop(0, width // tile, back_tile, 0)
    one_hot = (
        lax.broadcasted_iota(jnp.int32, (8, rows), 0) == tokr_ref[...]
    ).astype(F32).astype(BF16)

    def input_tile(i, carry):
        cols = pl.ds(pl.multiple_of(i * tile, tile), tile)
        grad = fwd_back[:, cols] + rev_back[:, cols]
        top = grad.astype(BF16)
        hout_ref[:, cols] = top
        left = grad - top.astype(F32)
        mid = left.astype(BF16)
        low = (left - mid.astype(F32)).astype(BF16)
        table = jnp.dot(one_hot, top, preferred_element_type=F32)
        table = table + jnp.dot(one_hot, mid, preferred_element_type=F32)
        table = table + jnp.dot(one_hot, low, preferred_element_type=F32)
        per = units // 2 // tile
        where = pl.ds(pl.multiple_of((i % per) * tile, tile), tile)
        at_rows = pl.ds(pl.multiple_of(8 + 8 * ((i // per) % 2), 8), 8)
        small[i // (2 * per), at_rows, where] = table
        return carry

    lax.fori_loop(0, width // tile, input_tile, 0)

    small_ids = [core_id, x_id] + bit_ids

    def small_copy(n):
        src = small.at[1 - ci] if n == 0 else small.at[2 + (n - 1) % 2]
        return remote(src, small_recv.at[n], s_ss.at[n], s_rs.at[n], small_ids[n])

    def small_last():
        return remote(small_ref.at[ci], small_ref.at[ci], s_ss.at[bits + 2], s_rs.at[bits + 2], core_id)

    def small_step(n):
        small_copy(n).wait_recv()
        base = small[ci] if n == 0 else small[2 + (n - 1) % 2]
        now = base + small_recv[n]
        if n < bits + 1:
            if n >= 2:
                small_copy(n - 1).wait_send()
            small[2 + n % 2] = now
            small_copy(n + 1).start()
        else:
            small_ref[ci] = now
            small_last().start()

    small_copy(0).start()

    def result_tile(i, carry):
        cols = pl.ds(pl.multiple_of(i * tile, tile), tile)
        mirror = pl.ds(pl.multiple_of(units - tile - i * tile, tile), tile)
        block_ref[:, cols] = (outs[:, cols] + mirrored(routs[:, mirror])).astype(BF16)
        return carry

    lax.fori_loop(0, units // tile, result_tile, 0)
    small_step(0)

    plans = [stages(j) for j in range(CHUNKS)]
    length = len(plans[0])
    small_at = 1
    for wave in range(length + CHUNKS - 1):
        for j in range(CHUNKS):
            if 0 <= wave - j < length:
                plans[j][wave - j]()
        if small_at < bits + 2:
            small_step(small_at)
            small_at += 1
    while small_at < bits + 2:
        small_step(small_at)
        small_at += 1
    small_last().wait_recv()

    for copy in sends:
        copy.wait_send()
    for j in range(CHUNKS):
        core_copy(j).wait_send()
        x_copy(j).wait_send()
        for b in range(bits):
            rs_copy(j, b).wait_send()
        for b in gathers:
            ag_copy(j, b).wait_send()
    small_copy(0).wait_send()
    small_copy(bits).wait_send()
    small_copy(bits + 1).wait_send()
    small_last().wait_send()


def local(seq_count, hidden, tokens, embedding, weight, kernel, cotangent):
    window, token_codes, upstream = hidden[0], tokens[0], cotangent[0]
    rows, width = window.shape
    depth, units = weight.shape
    blocks = width // depth
    taps, vocab = kernel.shape[0], embedding.shape[0]
    bits = seq_count.bit_length() - 1
    total = rows + 2 * EDGE
    cw = units // CHUNKS
    factor = 1.0 / math.sqrt(hidden.shape[0] * rows * lax.axis_size("dp") * lax.axis_size("seq"))
    stacked_rows = sum(size for size, _ in halvings(depth, bits))
    vmem = pl.BlockSpec(memory_space=pltpu.VMEM)
    dma = pltpu.SemaphoreType.DMA
    block_result, grad_hidden, grad_weight, sums = pl.pallas_call(
        functools.partial(body, seq_count, bits),
        out_shape=(
            jax.ShapeDtypeStruct((rows, units), BF16),
            jax.ShapeDtypeStruct((rows, width), BF16),
            jax.ShapeDtypeStruct((CHUNKS, depth, cw), BF16),
            jax.ShapeDtypeStruct((2, 24, units // 2), F32),
        ),
        in_specs=[vmem] * 7,
        out_specs=(vmem,) * 4,
        scratch_shapes=[
            pltpu.VMEM((blocks, depth, units), BF16),
            pltpu.VMEM((2, total, width), BF16),
            pltpu.VMEM((2, EDGE, width), BF16),
            pltpu.VMEM((2, total, units), BF16),
            pltpu.VMEM((2, EDGE, units), BF16),
            pltpu.VMEM((width, 2 * rows), BF16),
            pltpu.VMEM((2, total, units), F32),
            pltpu.VMEM((2, rows + 16, 128), F32),
            pltpu.VMEM((rows, units), F32),
            pltpu.VMEM((rows, units), BF16),
            pltpu.VMEM((2 * rows, units), BF16),
            pltpu.VMEM((rows, width), F32),
            pltpu.VMEM((rows, width), F32),
            pltpu.VMEM((CHUNKS, 2, depth, cw), F32),
            pltpu.VMEM((CHUNKS, depth, cw), F32),
            pltpu.VMEM((CHUNKS, 2, depth, cw), BF16),
            pltpu.VMEM((CHUNKS, 2, depth, cw), BF16),
            pltpu.VMEM((CHUNKS, depth, cw), BF16),
            pltpu.VMEM((CHUNKS, depth, cw), BF16),
            pltpu.VMEM((CHUNKS, stacked_rows, cw), BF16),
            pltpu.VMEM((CHUNKS, stacked_rows, cw), BF16),
            pltpu.VMEM((4, 24, units // 2), F32),
            pltpu.VMEM((bits + 2, 24, units // 2), F32),
            dma((4 * PIECES + 1,)), dma((4 * PIECES + 1,)),
            dma((4,)), dma((4,)),
            dma((CHUNKS, 2 + 2 * bits)), dma((CHUNKS, 2 + 2 * bits)),
            dma((bits + 3,)), dma((bits + 3,)),
        ],
        compiler_params=pltpu.CompilerParams(
            collective_id=0, has_side_effects=True, vmem_limit_bytes=48 * 1024 * 1024
        ),
        cost_estimate=pl.CostEstimate(
            flops=12 * rows * width * units, bytes_accessed=8 * rows * width, transcendentals=4 * rows * units
        ),
    )(
        window,
        token_codes.reshape(rows, 1),
        token_codes.reshape(1, rows),
        embedding,
        weight,
        kernel,
        upstream,
    )
    grad_weight = jnp.swapaxes(grad_weight, 0, 1).reshape(depth, units).astype(F32) * factor
    kernel_sum = jnp.concatenate([sums[0, :taps], sums[1, :taps]], axis=1) * factor
    table = jnp.concatenate([sums[0, 8 : 8 + vocab], sums[0, 16 : 16 + vocab], sums[1, 8 : 8 + vocab], sums[1, 16 : 16 + vocab]], axis=1)
    return (
        block_result[None],
        grad_hidden[None],
        grad_weight,
        kernel_sum,
        table * factor,
    )


def solution(mesh):
    in_specs = (P("dp", "seq", None), P("dp", "seq"), P(), P("dp", None), P(), P("dp", "seq", None))
    out_specs = (P("dp", "seq", None), P("dp", "seq", None), P("dp", None), P(), P())
    return jax.shard_map(
        functools.partial(local, mesh.shape["seq"]),
        mesh=mesh, in_specs=in_specs, out_specs=out_specs, check_vma=False,
    )
```

```python
import functools
import math

import jax
import jax.numpy as jnp
from jax import lax
from jax.experimental import pallas as pl
from jax.experimental.pallas import tpu as pltpu
from jax.sharding import PartitionSpec as P

MESH = pl.DeviceIdType.MESH
F32 = jnp.float32
BF16 = jnp.bfloat16
EDGE = 16
CHUNKS = 4
PIECES = 4
LANES = 256


def halvings(rows, bits):
    sizes = []
    for _ in range(bits):
        halved = rows // 2 >= 16 and rows % 32 == 0
        sizes.append((rows // 2 if halved else rows, halved))
        rows = sizes[-1][0]
    return sizes


def body(
    seq_count, bits, factor,
    hid_in, tok_in, emb_in, w_in, ker_in, cot_in,
    block_ref, hout_ref, gw_ref, kernel_ref, table_ref,
    hid_ref, tok_ref, emb_ref, ker_ref, cot_ref,
    wg, sx, hx, ux, hu, s2t, s2tp, val, gmix, outs, routs, gv, gvp, fwd_back, rev_back,
    acc, core_send, core_recv, seq_send, seq_recv, gathered,
    small, small_recv, small_ref,
    in_sems, w_ss, w_rs, h_ss, h_rs, r_ss, r_rs, s_ss, s_rs,
):
    rows = hid_ref.shape[0]
    depth, units = w_in.shape
    width = hid_ref.shape[1]
    taps = ker_ref.shape[0]
    reach = (taps - 1) // 2
    vocab = emb_ref.shape[0]
    total = rows + 2 * EDGE
    dp = lax.axis_index("dp")
    seq = lax.axis_index("seq")
    xi, ci = dp // 2, dp % 2
    loads = [
        pltpu.make_async_copy(src, dst, in_sems.at[n])
        for n, (src, dst) in enumerate(
            [(w_in, wg.at[dp]), (cot_in, cot_ref), (hid_in, hid_ref), (tok_in, tok_ref), (emb_in, emb_ref), (ker_in, ker_ref)]
        )
    ]
    for copy in loads:
        copy.start()
    core_id = (dp + 1 - 2 * ci, seq)
    x_id = (dp + 2 - 4 * xi, seq)
    bit_vals = [(seq // (1 << b)) % 2 for b in range(bits)]
    bit_ids = [(dp, seq + (1 - 2 * bit_vals[b]) * (1 << b)) for b in range(bits)]
    left_id = (dp, (seq + seq_count - 1) % seq_count)
    right_id = (dp, (seq + 1) % seq_count)

    partners = [core_id, x_id] + bit_ids + [left_id, right_id]
    barrier = pltpu.get_barrier_semaphore()
    for partner in partners:
        pl.semaphore_signal(barrier, inc=1, device_id=partner, device_id_type=MESH)
    pl.semaphore_wait(barrier, len(partners))

    def remote(src, dst, ss, rs, who):
        return pltpu.make_async_remote_copy(
            src_ref=src, dst_ref=dst, send_sem=ss, recv_sem=rs, device_id=who, device_id_type=MESH
        )

    yi = bit_vals[0]
    y_id = bit_ids[0]
    dpx = dp + 2 - 4 * xi
    half = depth // 2
    piece = half // PIECES

    def span(side, p):
        return pl.ds(pl.multiple_of(side * half + p * piece, 16), piece)

    sends = []
    over_x = [
        remote(wg.at[dp, span(yi, p)], wg.at[dp, span(yi, p)], w_ss.at[p], w_rs.at[p], x_id)
        for p in range(PIECES)
    ]
    loads[0].wait()
    for copy in over_x[:2]:
        copy.start()
    loads[1].wait()
    own = remote(wg.at[dp], wg.at[dp], w_ss.at[4 * PIECES], w_rs.at[4 * PIECES], core_id)
    own.start()
    sends += over_x + [own]
    halo_u = [
        remote(cot_ref.at[pl.ds(rows - EDGE, EDGE)], hu.at[0], h_ss.at[0], h_rs.at[0], right_id),
        remote(cot_ref.at[pl.ds(0, EDGE)], hu.at[1], h_ss.at[1], h_rs.at[1], left_id),
    ]
    for copy in halo_u:
        copy.start()

    tile = LANES
    for copy in loads[2:]:
        copy.wait()
    tok = jnp.broadcast_to(tok_ref[...], (rows, rows)).astype(F32).T
    tok = jnp.concatenate([tok] * (tile // rows), axis=1) if tile > rows else tok[:, :tile]

    def stream_tile(i, carry):
        cols = pl.ds(pl.multiple_of(i * tile, tile), tile)
        looked = jnp.zeros((rows, tile), F32)
        for k in range(vocab):
            looked = looked + jnp.where(tok == float(k), emb_ref[pl.ds(k, 1), cols], 0.0)
        sx[0, pl.ds(EDGE, rows), cols] = (hid_ref[:, cols].astype(F32) + looked).astype(BF16)
        return carry

    lax.fori_loop(0, width // tile, stream_tile, 0)
    halo_s = [
        remote(sx.at[0, pl.ds(rows, EDGE)], hx.at[0], h_ss.at[2], h_rs.at[2], right_id),
        remote(sx.at[0, pl.ds(EDGE, EDGE)], hx.at[1], h_ss.at[3], h_rs.at[3], left_id),
    ]
    for copy in halo_s:
        copy.start()
    sends += halo_u + halo_s

    has_left = (seq > 0).astype(F32)
    has_right = (seq < seq_count - 1).astype(F32)
    ux[0, pl.ds(EDGE, rows), :] = cot_ref[...]
    for copy in halo_u + halo_s:
        copy.wait_recv()
    sx[0, pl.ds(0, EDGE), :] = (hx[0].astype(F32) * has_left).astype(BF16)
    sx[0, pl.ds(rows + EDGE, EDGE), :] = (hx[1].astype(F32) * has_right).astype(BF16)
    ux[0, pl.ds(0, EDGE), :] = (hu[0].astype(F32) * has_left).astype(BF16)
    ux[0, pl.ds(rows + EDGE, EDGE), :] = (hu[1].astype(F32) * has_right).astype(BF16)

    flip = (
        lax.broadcasted_iota(jnp.int32, (tile, tile), 0)
        + lax.broadcasted_iota(jnp.int32, (tile, tile), 1)
        == tile - 1
    ).astype(F32).astype(BF16)

    def mirrored(block):
        return jnp.dot(block, flip, preferred_element_type=F32)

    def reverse_stream(i, carry):
        cols = pl.ds(pl.multiple_of(i * tile, tile), tile)
        back = pl.ds(pl.multiple_of(width - tile - i * tile, tile), tile)
        sx[1, :, back] = mirrored(sx[0, :, cols]).astype(BF16)
        return carry

    lax.fori_loop(0, width // tile, reverse_stream, 0)

    def reverse_up(i, carry):
        cols = pl.ds(pl.multiple_of(i * tile, tile), tile)
        back = pl.ds(pl.multiple_of(units - tile - i * tile, tile), tile)
        ux[1, :, back] = mirrored(ux[0, :, cols]).astype(BF16)
        return carry

    lax.fori_loop(0, units // tile, reverse_up, 0)

    def project(block, first):
        depth_cols = pl.ds(pl.multiple_of(block * depth, depth), depth)

        def project_tile(i, carry):
            cols = pl.ds(pl.multiple_of(i * tile, tile), tile)
            for s in range(2):
                part = jnp.dot(sx[s, :, depth_cols], wg[block, :, cols], preferred_element_type=F32)
                if first:
                    val[s, :, cols] = part
                else:
                    val[s, :, cols] += part
            return carry

        lax.fori_loop(0, units // tile, project_tile, 0)

    project(dp, True)

    over_y, over_core = [], []
    stream_copy = remote(
        s2t.at[pl.ds(pl.multiple_of((1 - xi) * 2 * depth, depth), 2 * depth)], s2tp, h_ss.at[4], h_rs.at[4], x_id
    )
    for p in range(PIECES):
        over_x[p].wait_recv()
        if p + 2 < PIECES:
            over_x[p + 2].start()
        over_y.append(
            remote(wg.at[dpx, span(yi, p)], wg.at[dpx, span(yi, p)], w_ss.at[PIECES + p], w_rs.at[PIECES + p], y_id)
        )
        over_core.append(
            remote(wg.at[dpx, span(yi, p)], wg.at[dpx, span(yi, p)], w_ss.at[2 * PIECES + p], w_rs.at[2 * PIECES + p], core_id)
        )
        over_y[p].start()
        over_core[p].start()
        if p == 0:
            own.wait_recv()
            project(dp + 1 - 2 * ci, False)

            def transpose_tile(i, carry):
                cols = pl.ds(pl.multiple_of(i * tile, tile), tile)
                for s in range(2):
                    s2t[cols, pl.ds(s * rows, rows)] = sx[s, pl.ds(EDGE, rows), cols].T
                return carry

            lax.fori_loop(0, width // tile, transpose_tile, 0)
    stream_copy.start()
    sends.append(stream_copy)
    over_core2 = []
    for p in range(PIECES):
        over_y[p].wait_recv()
        other = 1 - yi
        over_core2.append(
            remote(wg.at[dpx, span(other, p)], wg.at[dpx, span(other, p)], w_ss.at[3 * PIECES + p], w_rs.at[3 * PIECES + p], core_id)
        )
        over_core2[p].start()
    sends += over_y + over_core + over_core2
    for p in range(PIECES):
        over_core[p].wait_recv()
        over_core2[p].wait_recv()

    ew = 128
    cw = units // CHUNKS
    lo = EDGE - 8

    def strand_tile(i, carry):
        cols = pl.ds(pl.multiple_of(i * ew, ew), ew)
        tap_sums = [jnp.zeros((1, ew), F32)] * taps
        for s in range(2):
            val[s, :, cols] = val[s, :, cols].astype(BF16).astype(F32)
            wide = val[s, pl.ds(lo, rows + 16), cols]
            sig_wide = jax.nn.sigmoid(wide)
            gate_wide = wide * sig_wide
            gmix[s] = ux[s, :, cols].astype(F32)[lo : lo + rows + 16] * gate_wide
            lin, sig, gate = wide[8 : 8 + rows], sig_wide[8 : 8 + rows], gate_wide[8 : 8 + rows]
            up = ux[s, pl.ds(EDGE, rows), cols].astype(F32)
            mine = gmix[s, pl.ds(8, rows), :]
            mixing = jnp.zeros((rows, ew), F32)
            spread = jnp.zeros((rows, ew), F32)
            for m in range(taps):
                k = m if s == 0 else taps - 1 - m
                row = ker_ref[pl.ds(k, 1), cols]
                shifted = val[s, pl.ds(EDGE + m - reach, rows), cols]
                mixing = mixing + row * shifted
                tap_sums[k] = tap_sums[k] + jnp.sum(mine * shifted, axis=0, keepdims=True)
                spread = spread + row * gmix[s, pl.ds(8 + reach - m, rows), :]
            strand_out = mixing * gate
            if s == 0:
                outs[:, cols] = strand_out
            else:
                routs[:, cols] = strand_out.astype(BF16)
            grad = up * mixing * sig * (1.0 + lin * (1.0 - sig)) + spread
            inner = pl.ds(pl.multiple_of((i % (cw // ew)) * ew, ew), ew)
            gv[i // (cw // ew), pl.ds(s * rows, rows), inner] = grad.astype(BF16)
        small_cols = pl.ds(pl.multiple_of((i % (units // 2 // ew)) * ew, ew), ew)
        pad = [jnp.zeros((1, ew), F32)] * (8 - taps)
        small[i // (units // 2 // ew), pl.ds(0, 8), small_cols] = jnp.concatenate(tap_sums + pad, axis=0)
        return carry

    def elementwise(j):
        cols = pl.ds(j * cw, cw)
        for block in (dpx, dpx + 1 - 2 * ci):
            depth_cols = pl.ds(pl.multiple_of(block * depth, depth), depth)
            for s in range(2):
                val[s, :, cols] += jnp.dot(sx[s, :, depth_cols], wg[block, :, cols], preferred_element_type=F32)
        lax.fori_loop(j * (cw // ew), (j + 1) * (cw // ew), strand_tile, 0)
        grad_copy(j).start()

    def grad_copy(j):
        return remote(gv.at[j], gvp.at[j], r_ss.at[j, 1], r_rs.at[j, 1], x_id)

    levels = halvings(depth, bits)

    def core_copy(j):
        return remote(core_send.at[j], core_recv.at[j], r_ss.at[j, 0], r_rs.at[j, 0], core_id)

    def product(j):
        grad_copy(j).wait_recv()
        if j == 0:
            stream_copy.wait_recv()
        for side in range(2):
            block = 1 - ci if side == 0 else ci
            mine = pl.ds(pl.multiple_of((2 * xi + block) * depth, depth), depth)
            theirs = pl.ds(pl.multiple_of(block * depth, depth), depth)
            result = jnp.dot(s2t[mine, :], gv[j], preferred_element_type=F32)
            result = result + jnp.dot(s2tp[theirs, :], gvp[j], preferred_element_type=F32)
            if side == 0:
                core_send[j] = result.astype(BF16)
                core_copy(j).start()
            else:
                acc[j] = result

    def after_core(j):
        core_copy(j).wait_recv()
        acc[j] += core_recv[j].astype(F32)
        rs_start(j, 0)

    off = 0
    spans_keep, spans_send = [], []
    for (size, halved), bit in zip(levels, bit_vals):
        if halved:
            keep, give = off + bit * size, off + (1 - bit) * size
        else:
            keep, give = off, off
        spans_keep.append(pl.ds(pl.multiple_of(keep, 16), size))
        spans_send.append(pl.ds(pl.multiple_of(give, 16), size))
        off = keep
    sub_at = []
    at = 0
    for size, _ in levels:
        sub_at.append(at)
        at += size

    def rs_copy(j, b):
        where = pl.ds(sub_at[b], levels[b][0])
        return remote(seq_send.at[j, where], seq_recv.at[j, where], r_ss.at[j, 2 + b], r_rs.at[j, 2 + b], bit_ids[b])

    def rs_start(j, b):
        seq_send[j, pl.ds(sub_at[b], levels[b][0]), :] = acc[j, spans_send[b], :].astype(BF16)
        rs_copy(j, b).start()

    def rs_finish(j, b):
        rs_copy(j, b).wait_recv()
        acc[j, spans_keep[b], :] += seq_recv[j, pl.ds(sub_at[b], levels[b][0]), :].astype(F32)

    gathers = [b for b in reversed(range(bits)) if levels[b][1]]

    def ag_copy(j, b):
        ref = gathered.at[j, spans_keep[b]]
        return remote(ref, ref, r_ss.at[j, 2 + bits + b], r_rs.at[j, 2 + bits + b], bit_ids[b])

    def stages(j):
        def after_rs(b):
            rs_finish(j, b)
            if b + 1 < bits:
                rs_start(j, b + 1)
            else:
                gathered[j, spans_keep[-1], :] = acc[j, spans_keep[-1], :].astype(BF16)
                ag_copy(j, gathers[0]).start()

        def after_ag(n):
            ag_copy(j, gathers[n]).wait_recv()
            if n + 1 < len(gathers):
                ag_copy(j, gathers[n + 1]).start()
            else:
                gw_ref[:, pl.ds(j * cw, cw)] = gathered[j]

        steps = [functools.partial(stage, j) for stage in (elementwise, product, after_core)]
        steps += [functools.partial(after_rs, b) for b in range(bits)]
        steps += [functools.partial(after_ag, n) for n in range(len(gathers))]
        return steps

    def back_tile(i, carry):
        b = i // (depth // tile)
        r = pl.ds(pl.multiple_of((i % (depth // tile)) * tile, tile), tile)
        cols = pl.ds(pl.multiple_of(i * tile, tile), tile)
        mirror = pl.ds(pl.multiple_of(width - tile - i * tile, tile), tile)
        part = jnp.zeros((2 * rows, tile), F32)
        for j in range(CHUNKS):
            part = part + lax.dot_general(
                gv[j], wg[b, r, pl.ds(j * cw, cw)], (((1,), (1,)), ((), ())), preferred_element_type=F32
            )
        fwd_back[:, cols] = part[:rows]
        rev_back[:, mirror] = mirrored(part[rows:].astype(BF16))
        return carry

    one_hot = (
        lax.broadcasted_iota(jnp.int32, (8, rows), 0) == tok_ref[...]
    ).astype(F32).astype(BF16)

    def input_tile(i, carry):
        cols = pl.ds(pl.multiple_of(i * tile, tile), tile)
        grad = fwd_back[:, cols] + rev_back[:, cols]
        top = grad.astype(BF16)
        hout_ref[:, cols] = top
        left = grad - top.astype(F32)
        mid = left.astype(BF16)
        low = (left - mid.astype(F32)).astype(BF16)
        table = jnp.dot(one_hot, top, preferred_element_type=F32)
        table = table + jnp.dot(one_hot, mid, preferred_element_type=F32)
        table = table + jnp.dot(one_hot, low, preferred_element_type=F32)
        per = units // 2 // tile
        where = pl.ds(pl.multiple_of((i % per) * tile, tile), tile)
        at_rows = pl.ds(pl.multiple_of(8 + 8 * ((i // per) % 2), 8), 8)
        small[i // (2 * per), at_rows, where] = table
        return carry


    small_ids = [core_id, x_id] + bit_ids

    def small_copy(n):
        src = small.at[1 - ci] if n == 0 else small.at[2 + (n - 1) % 2]
        return remote(src, small_recv.at[n], s_ss.at[n], s_rs.at[n], small_ids[n])

    def small_last():
        return remote(small_ref.at[ci], small_ref.at[ci], s_ss.at[bits + 2], s_rs.at[bits + 2], core_id)

    def small_step(n):
        small_copy(n).wait_recv()
        base = small[ci] if n == 0 else small[2 + (n - 1) % 2]
        now = base + small_recv[n]
        if n < bits + 1:
            if n >= 2:
                small_copy(n - 1).wait_send()
            small[2 + n % 2] = now
            small_copy(n + 1).start()
        else:
            small_ref[ci] = now
            small_last().start()

    def result_tile(i, carry):
        cols = pl.ds(pl.multiple_of(i * tile, tile), tile)
        mirror = pl.ds(pl.multiple_of(units - tile - i * tile, tile), tile)
        block_ref[:, cols] = (outs[:, cols] + mirrored(routs[:, mirror])).astype(BF16)
        return carry

    tiles = width // tile

    def fill_back(part):
        lax.fori_loop(part * tiles // 2, (part + 1) * tiles // 2, back_tile, 0)

    def fill_input():
        lax.fori_loop(0, tiles, input_tile, 0)
        small_copy(0).start()

    def fill_result():
        lax.fori_loop(0, units // tile, result_tile, 0)
        small_step(0)

    def fill_back_input():
        fill_back(1)
        fill_input()

    fillers = [functools.partial(fill_back, 0), fill_back_input, fill_result]
    fillers += [functools.partial(small_step, n) for n in range(1, bits + 2)]

    plans = [stages(j) for j in range(CHUNKS)]
    length = len(plans[0])
    for wave in range(length + CHUNKS - 1):
        for j in range(CHUNKS):
            if 0 <= wave - j < length:
                plans[j][wave - j]()
        if wave >= CHUNKS and fillers:
            fillers.pop(0)()
    for filler in fillers:
        filler()
    small_last().wait_recv()
    for h in range(2):
        kernel_ref[:, pl.ds(h * units // 2, units // 2)] = small_ref[h, :taps, :] * factor
        for q in range(2):
            columns = pl.ds((2 * h + q) * (units // 2), units // 2)
            table_ref[:, columns] = small_ref[h, 8 + 8 * q : 8 + 8 * q + vocab, :] * factor

    for copy in sends:
        copy.wait_send()
    for j in range(CHUNKS):
        core_copy(j).wait_send()
        grad_copy(j).wait_send()
        for b in range(bits):
            rs_copy(j, b).wait_send()
        for b in gathers:
            ag_copy(j, b).wait_send()
    small_copy(0).wait_send()
    small_copy(bits).wait_send()
    small_copy(bits + 1).wait_send()
    small_last().wait_send()


def local(seq_count, hidden, tokens, embedding, weight, kernel, cotangent):
    window, token_codes, upstream = hidden[0], tokens[0], cotangent[0]
    rows, width = window.shape
    depth, units = weight.shape
    blocks = width // depth
    taps, vocab = kernel.shape[0], embedding.shape[0]
    bits = seq_count.bit_length() - 1
    positions = hidden.shape[0] * rows * lax.axis_size("dp") * seq_count
    total = rows + 2 * EDGE
    cw = units // CHUNKS
    factor = 1.0 / math.sqrt(positions)
    stacked_rows = sum(size for size, _ in halvings(depth, bits))
    vmem = pl.BlockSpec(memory_space=pltpu.VMEM)
    dma = pltpu.SemaphoreType.DMA
    block_result, grad_hidden, grad_weight, kernel_sum, table = pl.pallas_call(
        functools.partial(body, seq_count, bits, factor),
        out_shape=(
            jax.ShapeDtypeStruct((rows, units), BF16),
            jax.ShapeDtypeStruct((rows, width), BF16),
            jax.ShapeDtypeStruct((depth, units), BF16),
            jax.ShapeDtypeStruct((taps, units), F32),
            jax.ShapeDtypeStruct((vocab, width), F32),
        ),
        in_specs=[pl.BlockSpec(memory_space=pl.ANY)] * 6,
        out_specs=(vmem,) * 5,
        scratch_shapes=[
            pltpu.VMEM((rows, width), BF16),
            pltpu.VMEM((1, rows), jnp.int32),
            pltpu.VMEM((vocab, width), F32),
            pltpu.VMEM((taps, units), F32),
            pltpu.VMEM((rows, units), BF16),
            pltpu.VMEM((blocks, depth, units), BF16),
            pltpu.VMEM((2, total, width), BF16),
            pltpu.VMEM((2, EDGE, width), BF16),
            pltpu.VMEM((2, total, units), BF16),
            pltpu.VMEM((2, EDGE, units), BF16),
            pltpu.VMEM((width, 2 * rows), BF16),
            pltpu.VMEM((2 * depth, 2 * rows), BF16),
            pltpu.VMEM((2, total, units), F32),
            pltpu.VMEM((2, rows + 16, 128), F32),
            pltpu.VMEM((rows, units), F32),
            pltpu.VMEM((rows, units), BF16),
            pltpu.VMEM((CHUNKS, 2 * rows, cw), BF16),
            pltpu.VMEM((CHUNKS, 2 * rows, cw), BF16),
            pltpu.VMEM((rows, width), F32),
            pltpu.VMEM((rows, width), F32),
            pltpu.VMEM((CHUNKS, depth, cw), F32),
            pltpu.VMEM((CHUNKS, depth, cw), BF16),
            pltpu.VMEM((CHUNKS, depth, cw), BF16),
            pltpu.VMEM((CHUNKS, stacked_rows, cw), BF16),
            pltpu.VMEM((CHUNKS, stacked_rows, cw), BF16),
            pltpu.VMEM((CHUNKS, depth, cw), BF16),
            pltpu.VMEM((4, 24, units // 2), F32),
            pltpu.VMEM((bits + 2, 24, units // 2), F32),
            pltpu.VMEM((2, 24, units // 2), F32),
            dma((6,)),
            dma((4 * PIECES + 1,)), dma((4 * PIECES + 1,)),
            dma((5,)), dma((5,)),
            dma((CHUNKS, 2 + 2 * bits)), dma((CHUNKS, 2 + 2 * bits)),
            dma((bits + 3,)), dma((bits + 3,)),
        ],
        compiler_params=pltpu.CompilerParams(
            collective_id=0, has_side_effects=True, vmem_limit_bytes=48 * 1024 * 1024
        ),
        cost_estimate=pl.CostEstimate(
            flops=12 * rows * width * units, bytes_accessed=8 * rows * width, transcendentals=4 * rows * units
        ),
    )(
        window,
        token_codes.reshape(1, rows),
        embedding,
        weight,
        kernel,
        upstream,
    )
    grad_weight = grad_weight.astype(F32) * factor
    return (
        block_result[None],
        grad_hidden[None],
        grad_weight,
        kernel_sum,
        table,
    )


def solution(mesh):
    in_specs = (P("dp", "seq", None), P("dp", "seq"), P(), P("dp", None), P(), P("dp", "seq", None))
    out_specs = (P("dp", "seq", None), P("dp", "seq", None), P("dp", None), P(), P())
    return jax.shard_map(
        functools.partial(local, mesh.shape["seq"]),
        mesh=mesh, in_specs=in_specs, out_specs=out_specs, check_vma=False,
    )
```

```python
import functools
import math

import jax
import jax.numpy as jnp
from jax import lax
from jax.experimental import pallas as pl
from jax.experimental.pallas import tpu as pltpu
from jax.sharding import PartitionSpec as P

MESH = pl.DeviceIdType.MESH
F32 = jnp.float32
BF16 = jnp.bfloat16
EDGE = 16
CHUNKS = 4
PIECES = 4
LANES = 256


def level_plan(rows, bits):
    groups = [[0], [1, 2]] + [[b] for b in range(3, bits)] if bits >= 3 else [[b] for b in range(bits)]
    levels = []
    for group in groups:
        ways = 1 << len(group)
        split = rows % (16 * ways) == 0
        if split:
            rows //= ways
            levels.append((group, rows, True))
        else:
            levels += [([b], rows, False) for b in group]
    return levels


def body(
    seq_count, bits, factor,
    hid_in, tok_in, emb_in, w_in, ker_in, cot_in,
    block_ref, hout_ref, gw_ref, kernel_ref, table_ref,
    hid_ref, tok_ref, emb_ref, ker_ref, cot_ref,
    wg, sx, hx, ux, hu, s2t, s2tp, val, gmix, sigs, outs, routs, gv, gvp, fwd_back, rev_back,
    acc, core_send, core_recv, seq_send, seq_recv, gathered,
    small, small_recv, small_ref,
    in_sems, w_ss, w_rs, h_ss, h_rs, r_ss, r_rs, s_ss, s_rs,
):
    rows = hid_ref.shape[0]
    depth, units = w_in.shape
    width = hid_ref.shape[1]
    taps = ker_ref.shape[0]
    reach = (taps - 1) // 2
    vocab = emb_ref.shape[0]
    total = rows + 2 * EDGE
    dp = lax.axis_index("dp")
    seq = lax.axis_index("seq")
    xi, ci = dp // 2, dp % 2
    loads = [
        pltpu.make_async_copy(src, dst, in_sems.at[n])
        for n, (src, dst) in enumerate(
            [(w_in, wg.at[dp]), (cot_in, cot_ref), (hid_in, hid_ref), (tok_in, tok_ref), (emb_in, emb_ref), (ker_in, ker_ref)]
        )
    ]
    for copy in loads:
        copy.start()
    core_id = (dp + 1 - 2 * ci, seq)
    x_id = (dp + 2 - 4 * xi, seq)
    bit_vals = [(seq // (1 << b)) % 2 for b in range(bits)]
    bit_ids = [(dp, seq + (1 - 2 * bit_vals[b]) * (1 << b)) for b in range(bits)]
    left_id = (dp, (seq + seq_count - 1) % seq_count)
    right_id = (dp, (seq + 1) % seq_count)

    levels = level_plan(depth, bits)
    exchanges = [(n, d) for n, (group, _, _) in enumerate(levels) for d in range(1, 1 << len(group))]

    def peer_id(n, d):
        place = seq
        for at_bit, b in enumerate(levels[n][0]):
            if (d >> at_bit) & 1:
                place = place + (1 - 2 * bit_vals[b]) * (1 << b)
        return (dp, place)

    def digit(n, d):
        value = 0
        for at_bit, b in enumerate(levels[n][0]):
            bit = bit_vals[b]
            value = value + (1 - bit if (d >> at_bit) & 1 else bit) * (1 << at_bit)
        return value

    partners = [core_id, x_id] + [peer_id(n, d) for n, d in exchanges] + [left_id, right_id]
    barrier = pltpu.get_barrier_semaphore()
    for partner in partners:
        pl.semaphore_signal(barrier, inc=1, device_id=partner, device_id_type=MESH)
    pl.semaphore_wait(barrier, len(partners))

    def remote(src, dst, ss, rs, who):
        return pltpu.make_async_remote_copy(
            src_ref=src, dst_ref=dst, send_sem=ss, recv_sem=rs, device_id=who, device_id_type=MESH
        )

    yi = bit_vals[0]
    y_id = bit_ids[0]
    dpx = dp + 2 - 4 * xi
    half = depth // 2
    piece = half // PIECES

    def span(side, p):
        return pl.ds(pl.multiple_of(side * half + p * piece, 16), piece)

    sends = []
    over_x = [
        remote(wg.at[dp, span(yi, p)], wg.at[dp, span(yi, p)], w_ss.at[p], w_rs.at[p], x_id)
        for p in range(PIECES)
    ]
    loads[0].wait()
    for copy in over_x[:2]:
        copy.start()
    loads[1].wait()
    own = remote(wg.at[dp], wg.at[dp], w_ss.at[4 * PIECES], w_rs.at[4 * PIECES], core_id)
    own.start()
    sends += over_x + [own]
    halo_u = [
        remote(cot_ref.at[pl.ds(rows - EDGE, EDGE)], hu.at[0], h_ss.at[0], h_rs.at[0], right_id),
        remote(cot_ref.at[pl.ds(0, EDGE)], hu.at[1], h_ss.at[1], h_rs.at[1], left_id),
    ]
    for copy in halo_u:
        copy.start()

    tile = LANES
    for copy in loads[2:]:
        copy.wait()
    tok = jnp.broadcast_to(tok_ref[...], (rows, rows)).astype(F32).T
    tok = jnp.concatenate([tok] * (tile // rows), axis=1) if tile > rows else tok[:, :tile]

    def stream_tile(i, carry):
        cols = pl.ds(pl.multiple_of(i * tile, tile), tile)
        looked = jnp.zeros((rows, tile), F32)
        for k in range(vocab):
            looked = looked + jnp.where(tok == float(k), emb_ref[pl.ds(k, 1), cols], 0.0)
        sx[0, pl.ds(EDGE, rows), cols] = (hid_ref[:, cols].astype(F32) + looked).astype(BF16)
        return carry

    lax.fori_loop(0, width // tile, stream_tile, 0)
    halo_s = [
        remote(sx.at[0, pl.ds(rows, EDGE)], hx.at[0], h_ss.at[2], h_rs.at[2], right_id),
        remote(sx.at[0, pl.ds(EDGE, EDGE)], hx.at[1], h_ss.at[3], h_rs.at[3], left_id),
    ]
    for copy in halo_s:
        copy.start()
    sends += halo_u + halo_s

    over_y, over_core = [], []

    def arrived(p):
        over_x[p].wait_recv()
        if p + 2 < PIECES:
            over_x[p + 2].start()
        part = wg.at[dpx, span(yi, p)]
        over_y.append(remote(part, part, w_ss.at[PIECES + p], w_rs.at[PIECES + p], y_id))
        over_core.append(remote(part, part, w_ss.at[2 * PIECES + p], w_rs.at[2 * PIECES + p], core_id))
        over_y[p].start()
        over_core[p].start()

    has_left = (seq > 0).astype(F32)
    has_right = (seq < seq_count - 1).astype(F32)
    ux[0, pl.ds(EDGE, rows), :] = cot_ref[...]
    arrived(0)
    for copy in halo_u + halo_s:
        copy.wait_recv()
    sx[0, pl.ds(0, EDGE), :] = (hx[0].astype(F32) * has_left).astype(BF16)
    sx[0, pl.ds(rows + EDGE, EDGE), :] = (hx[1].astype(F32) * has_right).astype(BF16)
    ux[0, pl.ds(0, EDGE), :] = (hu[0].astype(F32) * has_left).astype(BF16)
    ux[0, pl.ds(rows + EDGE, EDGE), :] = (hu[1].astype(F32) * has_right).astype(BF16)

    arrived(1)

    flip = (
        lax.broadcasted_iota(jnp.int32, (tile, tile), 0)
        + lax.broadcasted_iota(jnp.int32, (tile, tile), 1)
        == tile - 1
    ).astype(F32).astype(BF16)

    def mirrored(block):
        return jnp.dot(block, flip, preferred_element_type=F32)

    def reverse_stream(i, carry):
        cols = pl.ds(pl.multiple_of(i * tile, tile), tile)
        back = pl.ds(pl.multiple_of(width - tile - i * tile, tile), tile)
        sx[1, :, back] = mirrored(sx[0, :, cols]).astype(BF16)
        return carry

    lax.fori_loop(0, width // tile, reverse_stream, 0)

    def reverse_up(i, carry):
        cols = pl.ds(pl.multiple_of(i * tile, tile), tile)
        back = pl.ds(pl.multiple_of(units - tile - i * tile, tile), tile)
        ux[1, :, back] = mirrored(ux[0, :, cols]).astype(BF16)
        return carry

    lax.fori_loop(0, units // tile, reverse_up, 0)

    def project(block, first):
        depth_cols = pl.ds(pl.multiple_of(block * depth, depth), depth)

        def project_tile(i, carry):
            cols = pl.ds(pl.multiple_of(i * tile, tile), tile)
            for s in range(2):
                part = jnp.dot(sx[s, :, depth_cols], wg[block, :, cols], preferred_element_type=F32)
                if first:
                    val[s, :, cols] = part
                else:
                    val[s, :, cols] += part
            return carry

        lax.fori_loop(0, units // tile, project_tile, 0)

    project(dp, True)

    arrived(2)
    own.wait_recv()
    project(dp + 1 - 2 * ci, False)

    def transpose_tile(i, carry):
        cols = pl.ds(pl.multiple_of(i * tile, tile), tile)
        for s in range(2):
            s2t[cols, pl.ds(s * rows, rows)] = sx[s, pl.ds(EDGE, rows), cols].T
        return carry

    lax.fori_loop(0, width // tile, transpose_tile, 0)
    for p in range(3, PIECES):
        arrived(p)
    stream_copy = remote(
        s2t.at[pl.ds(pl.multiple_of((1 - xi) * 2 * depth, depth), 2 * depth)], s2tp, h_ss.at[4], h_rs.at[4], x_id
    )
    stream_copy.start()
    sends.append(stream_copy)
    over_core2 = []
    for p in range(PIECES):
        over_y[p].wait_recv()
        other = 1 - yi
        over_core2.append(
            remote(wg.at[dpx, span(other, p)], wg.at[dpx, span(other, p)], w_ss.at[3 * PIECES + p], w_rs.at[3 * PIECES + p], core_id)
        )
        over_core2[p].start()
    sends += over_y + over_core + over_core2
    for p in range(PIECES):
        over_core[p].wait_recv()
        over_core2[p].wait_recv()

    ew = 128
    cw = units // CHUNKS
    lo = EDGE - 8

    rt = 32

    def strand_tile(i, carry):
        cols = pl.ds(pl.multiple_of(i * ew, ew), ew)
        inner = pl.ds(pl.multiple_of((i % (cw // ew)) * ew, ew), ew)
        tap_rows = [ker_ref[pl.ds(k, 1), cols] for k in range(taps)]
        tap_sums = [jnp.zeros((8, ew), F32)] * taps
        for s in range(2):
            for r in range(0, rows + 16, rt // 2):
                at = pl.ds(lo + r, rt // 2)
                part = val[s, at, cols].astype(BF16).astype(F32)
                val[s, at, cols] = part
                logistic = jax.nn.sigmoid(part)
                gate = part * logistic
                sigs[s, pl.ds(r, rt // 2), :] = logistic
                gmix[s, pl.ds(r, rt // 2), :] = ux[s, at, cols].astype(F32) * gate
            for r in range(0, rows, rt):
                lin = val[s, pl.ds(EDGE + r, rt), cols]
                sig = sigs[s, pl.ds(8 + r, rt), :]
                up = ux[s, pl.ds(EDGE + r, rt), cols].astype(F32)
                mine = gmix[s, pl.ds(8 + r, rt), :]
                mixing = jnp.zeros((rt, ew), F32)
                spread = jnp.zeros((rt, ew), F32)
                for m in range(taps):
                    k = m if s == 0 else taps - 1 - m
                    row = tap_rows[k]
                    shifted = val[s, pl.ds(EDGE + r + m - reach, rt), cols]
                    mixing = mixing + row * shifted
                    product_sum = mine * shifted
                    for q in range(0, rt, 8):
                        tap_sums[k] = tap_sums[k] + product_sum[q : q + 8]
                    spread = spread + row * gmix[s, pl.ds(8 + r + reach - m, rt), :]
                strand_out = mixing * (lin * sig)
                if s == 0:
                    outs[pl.ds(r, rt), cols] = strand_out
                else:
                    routs[pl.ds(r, rt), cols] = strand_out.astype(BF16)
                grad = up * mixing * sig * (1.0 + lin * (1.0 - sig)) + spread
                gv[i // (cw // ew), pl.ds(s * rows + r, rt), inner] = grad.astype(BF16)
        tap_sums = [jnp.sum(value, axis=0, keepdims=True) for value in tap_sums]
        small_cols = pl.ds(pl.multiple_of((i % (units // 2 // ew)) * ew, ew), ew)
        pad = [jnp.zeros((1, ew), F32)] * (8 - taps)
        small[i // (units // 2 // ew), pl.ds(0, 8), small_cols] = jnp.concatenate(tap_sums + pad, axis=0)
        return carry

    def elementwise(j):
        cols = pl.ds(j * cw, cw)
        for block in (dpx, dpx + 1 - 2 * ci):
            depth_cols = pl.ds(pl.multiple_of(block * depth, depth), depth)
            for s in range(2):
                val[s, :, cols] += jnp.dot(sx[s, :, depth_cols], wg[block, :, cols], preferred_element_type=F32)
        lax.fori_loop(j * (cw // ew), (j + 1) * (cw // ew), strand_tile, 0)
        grad_copy(j).start()

    def grad_copy(j):
        return remote(gv.at[j], gvp.at[j], r_ss.at[j, 1], r_rs.at[j, 1], x_id)

    def core_copy(j):
        return remote(core_send.at[j], core_recv.at[j], r_ss.at[j, 0], r_rs.at[j, 0], core_id)

    def product(j):
        grad_copy(j).wait_recv()
        if j == 0:
            stream_copy.wait_recv()
        for side in range(2):
            block = 1 - ci if side == 0 else ci
            mine = pl.ds(pl.multiple_of((2 * xi + block) * depth, depth), depth)
            theirs = pl.ds(pl.multiple_of(block * depth, depth), depth)
            result = jnp.dot(s2t[mine, :], gv[j], preferred_element_type=F32)
            result = result + jnp.dot(s2tp[theirs, :], gvp[j], preferred_element_type=F32)
            if side == 0:
                core_send[j] = result.astype(BF16)
                core_copy(j).start()
            else:
                acc[j] = result

    def after_core(j):
        core_copy(j).wait_recv()
        acc[j] += core_recv[j].astype(F32)
        rs_start(j, 0)

    bases = [0]
    for n, (_, size, split) in enumerate(levels):
        bases.append(bases[-1] + digit(n, 0) * size if split else bases[-1])

    def rows_at(n, d):
        size, split = levels[n][1:]
        base = bases[n] + digit(n, d) * size if split else bases[n]
        return pl.ds(pl.multiple_of(base, 16), size)

    slots, at = {}, 0
    for n, d in exchanges:
        slots[n, d] = at
        at += levels[n][1]
    number = {pair: k for k, pair in enumerate(exchanges)}
    ways = [[d for m, d in exchanges if m == n] for n in range(len(levels))]

    def rs_copy(j, n, d):
        where = pl.ds(slots[n, d], levels[n][1])
        sem = 2 + number[n, d]
        return remote(seq_send.at[j, where], seq_recv.at[j, where], r_ss.at[j, sem], r_rs.at[j, sem], peer_id(n, d))

    def rs_start(j, n):
        for d in ways[n]:
            seq_send[j, pl.ds(slots[n, d], levels[n][1]), :] = acc[j, rows_at(n, d), :].astype(BF16)
            rs_copy(j, n, d).start()

    def rs_finish(j, n):
        for d in ways[n]:
            rs_copy(j, n, d).wait_recv()
        total_rows = acc[j, rows_at(n, 0), :]
        for d in ways[n]:
            total_rows = total_rows + seq_recv[j, pl.ds(slots[n, d], levels[n][1]), :].astype(F32)
        acc[j, rows_at(n, 0), :] = total_rows

    gathers = [n for n in reversed(range(len(levels))) if levels[n][2]]

    def ag_copy(j, n, d):
        size = levels[n][1]
        ref = gathered.at[j, pl.ds(pl.multiple_of(bases[n + 1], 16), size)]
        sem = 2 + len(exchanges) + number[n, d]
        return remote(ref, ref, r_ss.at[j, sem], r_rs.at[j, sem], peer_id(n, d))

    def ag_start(j, n):
        for d in ways[n]:
            ag_copy(j, n, d).start()

    def stages(j):
        def after_rs(n):
            rs_finish(j, n)
            if n + 1 < len(levels):
                rs_start(j, n + 1)
            else:
                last = rows_at(n, 0)
                gathered[j, last, :] = acc[j, last, :].astype(BF16)
                ag_start(j, gathers[0])

        def after_ag(k):
            for d in ways[gathers[k]]:
                ag_copy(j, gathers[k], d).wait_recv()
            if k + 1 < len(gathers):
                ag_start(j, gathers[k + 1])
            else:
                gw_ref[:, pl.ds(j * cw, cw)] = gathered[j]

        steps = [functools.partial(stage, j) for stage in (elementwise, product, after_core)]
        steps += [functools.partial(after_rs, b) for b in range(len(levels))]
        steps += [functools.partial(after_ag, n) for n in range(len(gathers))]
        return steps

    def back_tile(i, carry):
        b = i // (depth // tile)
        r = pl.ds(pl.multiple_of((i % (depth // tile)) * tile, tile), tile)
        cols = pl.ds(pl.multiple_of(i * tile, tile), tile)
        mirror = pl.ds(pl.multiple_of(width - tile - i * tile, tile), tile)
        part = jnp.zeros((2 * rows, tile), F32)
        for j in range(CHUNKS):
            part = part + lax.dot_general(
                gv[j], wg[b, r, pl.ds(j * cw, cw)], (((1,), (1,)), ((), ())), preferred_element_type=F32
            )
        fwd_back[:, cols] = part[:rows]
        rev_back[:, mirror] = mirrored(part[rows:].astype(BF16))
        return carry

    one_hot = (
        lax.broadcasted_iota(jnp.int32, (8, rows), 0) == tok_ref[...]
    ).astype(F32).astype(BF16)

    def input_tile(i, carry):
        cols = pl.ds(pl.multiple_of(i * tile, tile), tile)
        grad = fwd_back[:, cols] + rev_back[:, cols]
        top = grad.astype(BF16)
        hout_ref[:, cols] = top
        left = grad - top.astype(F32)
        mid = left.astype(BF16)
        low = (left - mid.astype(F32)).astype(BF16)
        table = jnp.dot(one_hot, top, preferred_element_type=F32)
        table = table + jnp.dot(one_hot, mid, preferred_element_type=F32)
        table = table + jnp.dot(one_hot, low, preferred_element_type=F32)
        per = units // 2 // tile
        where = pl.ds(pl.multiple_of((i % per) * tile, tile), tile)
        at_rows = pl.ds(pl.multiple_of(8 + 8 * ((i // per) % 2), 8), 8)
        small[i // (2 * per), at_rows, where] = table
        return carry


    small_ids = [core_id, x_id] + bit_ids

    def small_copy(n):
        src = small.at[1 - ci] if n == 0 else small.at[2 + (n - 1) % 2]
        return remote(src, small_recv.at[n], s_ss.at[n], s_rs.at[n], small_ids[n])

    def small_last():
        return remote(small_ref.at[ci], small_ref.at[ci], s_ss.at[bits + 2], s_rs.at[bits + 2], core_id)

    def small_step(n):
        small_copy(n).wait_recv()
        base = small[ci] if n == 0 else small[2 + (n - 1) % 2]
        now = base + small_recv[n]
        if n < bits + 1:
            if n >= 2:
                small_copy(n - 1).wait_send()
            small[2 + n % 2] = now
            small_copy(n + 1).start()
        else:
            small_ref[ci] = now
            small_last().start()

    def result_tile(i, carry):
        cols = pl.ds(pl.multiple_of(i * tile, tile), tile)
        mirror = pl.ds(pl.multiple_of(units - tile - i * tile, tile), tile)
        block_ref[:, cols] = (outs[:, cols] + mirrored(routs[:, mirror])).astype(BF16)
        return carry

    tiles = width // tile

    def fill_back(part):
        lax.fori_loop(part * tiles // 4, (part + 1) * tiles // 4, back_tile, 0)

    def fill_input():
        lax.fori_loop(0, tiles, input_tile, 0)
        small_copy(0).start()

    def fill_result():
        lax.fori_loop(0, units // tile, result_tile, 0)
        small_step(0)

    fillers = [functools.partial(fill_back, part) for part in range(4)] + [fill_input, fill_result]
    fillers += [functools.partial(small_step, n) for n in range(1, bits + 2)]

    plans = [stages(j) for j in range(CHUNKS)]
    length = len(plans[0])
    for wave in range(length + CHUNKS - 1):
        if wave < CHUNKS:
            plans[wave][0]()
        for j in range(CHUNKS):
            if 1 <= wave - j < length:
                plans[j][wave - j]()
                if wave >= CHUNKS and fillers:
                    fillers.pop(0)()
    for filler in fillers:
        filler()
    small_last().wait_recv()
    for h in range(2):
        kernel_ref[:, pl.ds(h * units // 2, units // 2)] = small_ref[h, :taps, :] * factor
        for q in range(2):
            columns = pl.ds((2 * h + q) * (units // 2), units // 2)
            table_ref[:, columns] = small_ref[h, 8 + 8 * q : 8 + 8 * q + vocab, :] * factor

    for copy in sends:
        copy.wait_send()
    for j in range(CHUNKS):
        core_copy(j).wait_send()
        grad_copy(j).wait_send()
        for n, d in exchanges:
            rs_copy(j, n, d).wait_send()
            if levels[n][2]:
                ag_copy(j, n, d).wait_send()
    small_copy(0).wait_send()
    small_copy(bits).wait_send()
    small_copy(bits + 1).wait_send()
    small_last().wait_send()


def finish(factor, b_in, h_in, g_in, k_in, t_in, b_out, h_out, g_out, k_out, t_out, narrow, wide, sems):
    copies = [
        pltpu.make_async_copy(src, dst, sems.at[n])
        for n, (src, dst) in enumerate([(h_in, h_out), (b_in, b_out), (k_in, k_out), (t_in, t_out)])
    ]
    step = g_in.shape[0] // 4
    parts = [pl.ds(q * step, step) for q in range(4)]
    fetches = [pltpu.make_async_copy(g_in.at[part], narrow.at[part], sems.at[8 + q]) for q, part in enumerate(parts)]
    for copy in fetches:
        copy.start()
    for copy in copies:
        copy.start()
    for q, part in enumerate(parts):
        fetches[q].wait()
        wide[part, :] = narrow[part, :].astype(F32) * factor
        copies.append(pltpu.make_async_copy(wide.at[part], g_out.at[part], sems.at[4 + q]))
        copies[-1].start()
    for copy in copies:
        copy.wait()


def local(seq_count, hidden, tokens, embedding, weight, kernel, cotangent):
    window, token_codes, upstream = hidden[0], tokens[0], cotangent[0]
    rows, width = window.shape
    depth, units = weight.shape
    blocks = width // depth
    taps, vocab = kernel.shape[0], embedding.shape[0]
    bits = seq_count.bit_length() - 1
    positions = hidden.shape[0] * rows * lax.axis_size("dp") * seq_count
    total = rows + 2 * EDGE
    cw = units // CHUNKS
    factor = 1.0 / math.sqrt(positions)
    levels = level_plan(depth, bits)
    stacked_rows = sum(size * ((1 << len(group)) - 1) for group, size, _ in levels)
    copies = sum((1 << len(group)) - 1 for group, _, _ in levels)
    vmem = pl.BlockSpec(memory_space=pltpu.VMEM)
    dma = pltpu.SemaphoreType.DMA
    block_result, grad_hidden, grad_weight, kernel_sum, table = pl.pallas_call(
        functools.partial(body, seq_count, bits, factor),
        out_shape=(
            jax.ShapeDtypeStruct((rows, units), BF16),
            jax.ShapeDtypeStruct((rows, width), BF16),
            jax.ShapeDtypeStruct((depth, units), BF16),
            jax.ShapeDtypeStruct((taps, units), F32),
            jax.ShapeDtypeStruct((vocab, width), F32),
        ),
        in_specs=[pl.BlockSpec(memory_space=pltpu.HBM)] * 6,
        out_specs=(vmem,) * 5,
        scratch_shapes=[
            pltpu.VMEM((rows, width), BF16),
            pltpu.VMEM((1, rows), jnp.int32),
            pltpu.VMEM((vocab, width), F32),
            pltpu.VMEM((taps, units), F32),
            pltpu.VMEM((rows, units), BF16),
            pltpu.VMEM((blocks, depth, units), BF16),
            pltpu.VMEM((2, total, width), BF16),
            pltpu.VMEM((2, EDGE, width), BF16),
            pltpu.VMEM((2, total, units), BF16),
            pltpu.VMEM((2, EDGE, units), BF16),
            pltpu.VMEM((width, 2 * rows), BF16),
            pltpu.VMEM((2 * depth, 2 * rows), BF16),
            pltpu.VMEM((2, total, units), F32),
            pltpu.VMEM((2, rows + 16, 128), F32),
            pltpu.VMEM((2, rows + 16, 128), F32),
            pltpu.VMEM((rows, units), F32),
            pltpu.VMEM((rows, units), BF16),
            pltpu.VMEM((CHUNKS, 2 * rows, cw), BF16),
            pltpu.VMEM((CHUNKS, 2 * rows, cw), BF16),
            pltpu.VMEM((rows, width), F32),
            pltpu.VMEM((rows, width), F32),
            pltpu.VMEM((CHUNKS, depth, cw), F32),
            pltpu.VMEM((CHUNKS, depth, cw), BF16),
            pltpu.VMEM((CHUNKS, depth, cw), BF16),
            pltpu.VMEM((CHUNKS, stacked_rows, cw), BF16),
            pltpu.VMEM((CHUNKS, stacked_rows, cw), BF16),
            pltpu.VMEM((CHUNKS, depth, cw), BF16),
            pltpu.VMEM((4, 24, units // 2), F32),
            pltpu.VMEM((bits + 2, 24, units // 2), F32),
            pltpu.VMEM((2, 24, units // 2), F32),
            dma((6,)),
            dma((4 * PIECES + 1,)), dma((4 * PIECES + 1,)),
            dma((5,)), dma((5,)),
            dma((CHUNKS, 2 + 2 * copies)), dma((CHUNKS, 2 + 2 * copies)),
            dma((bits + 3,)), dma((bits + 3,)),
        ],
        compiler_params=pltpu.CompilerParams(
            collective_id=0, has_side_effects=True, vmem_limit_bytes=60 * 1024 * 1024
        ),
        cost_estimate=pl.CostEstimate(
            flops=12 * rows * width * units, bytes_accessed=8 * rows * width, transcendentals=4 * rows * units
        ),
    )(
        window,
        token_codes.reshape(1, rows),
        embedding,
        weight,
        kernel,
        upstream,
    )
    block_result, grad_hidden, grad_weight, kernel_sum, table = pl.pallas_call(
        functools.partial(finish, factor),
        out_shape=(
            jax.ShapeDtypeStruct((rows, units), BF16),
            jax.ShapeDtypeStruct((rows, width), BF16),
            jax.ShapeDtypeStruct((depth, units), F32),
            jax.ShapeDtypeStruct((taps, units), F32),
            jax.ShapeDtypeStruct((vocab, width), F32),
        ),
        in_specs=[pl.BlockSpec(memory_space=pltpu.HBM)] * 5,
        out_specs=(pl.BlockSpec(memory_space=pltpu.HBM),) * 5,
        scratch_shapes=[pltpu.VMEM((depth, units), BF16), pltpu.VMEM((depth, units), F32), dma((12,))],
        compiler_params=pltpu.CompilerParams(vmem_limit_bytes=60 * 1024 * 1024),
    )(block_result, grad_hidden, grad_weight, kernel_sum, table)
    return (
        block_result[None],
        grad_hidden[None],
        grad_weight,
        kernel_sum,
        table,
    )


def solution(mesh):
    in_specs = (P("dp", "seq", None), P("dp", "seq"), P(), P("dp", None), P(), P("dp", "seq", None))
    out_specs = (P("dp", "seq", None), P("dp", "seq", None), P("dp", None), P(), P())
    return jax.shard_map(
        functools.partial(local, mesh.shape["seq"]),
        mesh=mesh, in_specs=in_specs, out_specs=out_specs, check_vma=False,
    )
```

```python
import functools
import math

import jax
import jax.numpy as jnp
from jax import lax
from jax.experimental import pallas as pl
from jax.experimental.pallas import tpu as pltpu
from jax.sharding import PartitionSpec as P

MESH = pl.DeviceIdType.MESH
F32 = jnp.float32
BF16 = jnp.bfloat16
EDGE = 16
CHUNKS = 4
LANES = 256


def level_plan(rows, bits):
    groups = [[0], [1, 2]] + [[b] for b in range(3, bits)] if bits >= 3 else [[b] for b in range(bits)]
    levels = []
    for group in groups:
        ways = 1 << len(group)
        split = rows % (16 * ways) == 0
        if split:
            rows //= ways
            levels.append((group, rows, True))
        else:
            levels += [([b], rows, False) for b in group]
    return levels


def body(
    seq_count, bits, factor,
    hid_in, tok_in, emb_in, w_in, ker_in, cot_in,
    block_ref, hout_ref, gw_ref, kernel_ref, table_ref,
    hid_ref, tok_ref, emb_ref, ker_ref, cot_ref,
    wg, sx, hx, ux, hu, s2t, s2tp, val, gmix, sigs, outs, routs, gv, gvp, fwd_back, rev_back,
    acc, core_send, core_recv, seq_send, seq_recv, gathered,
    small, small_recv, small_ref,
    in_sems, w_ss, w_rs, h_ss, h_rs, r_ss, r_rs, s_ss, s_rs,
):
    rows = hid_ref.shape[0]
    depth, units = w_in.shape
    width = hid_ref.shape[1]
    taps = ker_ref.shape[0]
    reach = (taps - 1) // 2
    vocab = emb_ref.shape[0]
    total = rows + 2 * EDGE
    dp = lax.axis_index("dp")
    seq = lax.axis_index("seq")
    xi, ci = dp // 2, dp % 2
    cw = units // CHUNKS
    w_loads = [
        pltpu.make_async_copy(w_in.at[:, pl.ds(p * cw, cw)], wg.at[p, dp], in_sems.at[5 + p]) for p in range(CHUNKS)
    ]
    loads = [
        pltpu.make_async_copy(src, dst, in_sems.at[n])
        for n, (src, dst) in enumerate(
            [(cot_in, cot_ref), (hid_in, hid_ref), (tok_in, tok_ref), (emb_in, emb_ref), (ker_in, ker_ref)]
        )
    ]
    for copy in w_loads + loads:
        copy.start()
    core_id = (dp + 1 - 2 * ci, seq)
    x_id = (dp + 2 - 4 * xi, seq)
    bit_vals = [(seq // (1 << b)) % 2 for b in range(bits)]
    bit_ids = [(dp, seq + (1 - 2 * bit_vals[b]) * (1 << b)) for b in range(bits)]
    left_id = (dp, (seq + seq_count - 1) % seq_count)
    right_id = (dp, (seq + 1) % seq_count)

    levels = level_plan(depth, bits)
    exchanges = [(n, d) for n, (group, _, _) in enumerate(levels) for d in range(1, 1 << len(group))]

    def peer_id(n, d):
        place = seq
        for at_bit, b in enumerate(levels[n][0]):
            if (d >> at_bit) & 1:
                place = place + (1 - 2 * bit_vals[b]) * (1 << b)
        return (dp, place)

    def digit(n, d):
        value = 0
        for at_bit, b in enumerate(levels[n][0]):
            bit = bit_vals[b]
            value = value + (1 - bit if (d >> at_bit) & 1 else bit) * (1 << at_bit)
        return value

    partners = [core_id, x_id] + [peer_id(n, d) for n, d in exchanges] + [left_id, right_id]
    barrier = pltpu.get_barrier_semaphore()
    for partner in partners:
        pl.semaphore_signal(barrier, inc=1, device_id=partner, device_id_type=MESH)
    pl.semaphore_wait(barrier, len(partners))

    def remote(src, dst, ss, rs, who):
        return pltpu.make_async_remote_copy(
            src_ref=src, dst_ref=dst, send_sem=ss, recv_sem=rs, device_id=who, device_id_type=MESH
        )

    yi = bit_vals[0]
    y_id = bit_ids[0]
    dpx = dp + 2 - 4 * xi
    half = depth // 2

    def part_of(p, block, side):
        return wg.at[p, block, pl.ds(pl.multiple_of(side * half, 16), half)]

    def passed(p, block, side, sem, who):
        part = wg.at[p, block] if side is None else part_of(p, block, side)
        return remote(part, part, w_ss.at[sem * CHUNKS + p], w_rs.at[sem * CHUNKS + p], who)

    over_x = [passed(p, dp, yi, 0, x_id) for p in range(CHUNKS)]
    own = [passed(p, dp, None, 1, core_id) for p in range(CHUNKS)]
    over_y = [passed(p, dpx, yi, 2, y_id) for p in range(CHUNKS)]
    over_core = [passed(p, dpx, yi, 3, core_id) for p in range(CHUNKS)]
    over_core2 = [passed(p, dpx, 1 - yi, 4, core_id) for p in range(CHUNKS)]
    for p in range(CHUNKS):
        w_loads[p].wait()
        over_x[p].start()
        own[p].start()
    loads[0].wait()
    sends = over_x + own + over_y + over_core + over_core2
    halo_u = [
        remote(cot_ref.at[pl.ds(rows - EDGE, EDGE)], hu.at[0], h_ss.at[0], h_rs.at[0], right_id),
        remote(cot_ref.at[pl.ds(0, EDGE)], hu.at[1], h_ss.at[1], h_rs.at[1], left_id),
    ]
    for copy in halo_u:
        copy.start()

    tile = LANES
    for copy in loads[1:]:
        copy.wait()
    tok = jnp.broadcast_to(tok_ref[...], (rows, rows)).astype(F32).T
    tok = jnp.concatenate([tok] * (tile // rows), axis=1) if tile > rows else tok[:, :tile]

    def stream_tile(i, carry):
        cols = pl.ds(pl.multiple_of(i * tile, tile), tile)
        looked = jnp.zeros((rows, tile), F32)
        for k in range(vocab):
            looked = looked + jnp.where(tok == float(k), emb_ref[pl.ds(k, 1), cols], 0.0)
        sx[0, pl.ds(EDGE, rows), cols] = (hid_ref[:, cols].astype(F32) + looked).astype(BF16)
        return carry

    lax.fori_loop(0, width // tile, stream_tile, 0)
    halo_s = [
        remote(sx.at[0, pl.ds(rows, EDGE)], hx.at[0], h_ss.at[2], h_rs.at[2], right_id),
        remote(sx.at[0, pl.ds(EDGE, EDGE)], hx.at[1], h_ss.at[3], h_rs.at[3], left_id),
    ]
    for copy in halo_s:
        copy.start()
    sends += halo_u + halo_s

    has_left = (seq > 0).astype(F32)
    has_right = (seq < seq_count - 1).astype(F32)
    ux[0, pl.ds(EDGE, rows), :] = cot_ref[...]
    for copy in halo_u + halo_s:
        copy.wait_recv()
    sx[0, pl.ds(0, EDGE), :] = (hx[0].astype(F32) * has_left).astype(BF16)
    sx[0, pl.ds(rows + EDGE, EDGE), :] = (hx[1].astype(F32) * has_right).astype(BF16)
    ux[0, pl.ds(0, EDGE), :] = (hu[0].astype(F32) * has_left).astype(BF16)
    ux[0, pl.ds(rows + EDGE, EDGE), :] = (hu[1].astype(F32) * has_right).astype(BF16)

    flip = (
        lax.broadcasted_iota(jnp.int32, (tile, tile), 0)
        + lax.broadcasted_iota(jnp.int32, (tile, tile), 1)
        == tile - 1
    ).astype(F32).astype(BF16)

    def mirrored(block):
        return jnp.dot(block, flip, preferred_element_type=F32)

    def reverse_stream(i, carry):
        cols = pl.ds(pl.multiple_of(i * tile, tile), tile)
        back = pl.ds(pl.multiple_of(width - tile - i * tile, tile), tile)
        sx[1, :, back] = mirrored(sx[0, :, cols]).astype(BF16)
        return carry

    lax.fori_loop(0, width // tile, reverse_stream, 0)

    def reverse_up(i, carry):
        cols = pl.ds(pl.multiple_of(i * tile, tile), tile)
        back = pl.ds(pl.multiple_of(units - tile - i * tile, tile), tile)
        ux[1, :, back] = mirrored(ux[0, :, cols]).astype(BF16)
        return carry

    lax.fori_loop(0, units // tile, reverse_up, 0)

    def arrived_x(p):
        over_x[p].wait_recv()
        over_y[p].start()
        over_core[p].start()
        if p == CHUNKS - 1:
            stream_copy.start()

    def arrived_y(p):
        over_y[p].wait_recv()
        over_core2[p].start()

    def transpose_tile(i, carry):
        cols = pl.ds(pl.multiple_of(i * tile, tile), tile)
        for s in range(2):
            s2t[cols, pl.ds(s * rows, rows)] = sx[s, pl.ds(EDGE, rows), cols].T
        return carry

    lax.fori_loop(0, width // tile, transpose_tile, 0)
    stream_copy = remote(
        s2t.at[pl.ds(pl.multiple_of((1 - xi) * 2 * depth, depth), 2 * depth)], s2tp, h_ss.at[4], h_rs.at[4], x_id
    )
    sends.append(stream_copy)

    ew = 128
    lo = EDGE - 8

    rt = 32

    def strand_tile(i, carry):
        cols = pl.ds(pl.multiple_of(i * ew, ew), ew)
        inner = pl.ds(pl.multiple_of((i % (cw // ew)) * ew, ew), ew)
        tap_rows = [ker_ref[pl.ds(k, 1), cols] for k in range(taps)]
        tap_sums = [jnp.zeros((8, ew), F32)] * taps
        for s in range(2):
            for r in range(0, rows + 16, rt // 2):
                at = pl.ds(lo + r, rt // 2)
                part = val[s, at, cols].astype(BF16).astype(F32)
                val[s, at, cols] = part
                logistic = jax.nn.sigmoid(part)
                gate = part * logistic
                sigs[s, pl.ds(r, rt // 2), :] = logistic
                gmix[s, pl.ds(r, rt // 2), :] = ux[s, at, cols].astype(F32) * gate
            for r in range(0, rows, rt):
                lin = val[s, pl.ds(EDGE + r, rt), cols]
                sig = sigs[s, pl.ds(8 + r, rt), :]
                up = ux[s, pl.ds(EDGE + r, rt), cols].astype(F32)
                mine = gmix[s, pl.ds(8 + r, rt), :]
                mixing = jnp.zeros((rt, ew), F32)
                spread = jnp.zeros((rt, ew), F32)
                for m in range(taps):
                    k = m if s == 0 else taps - 1 - m
                    row = tap_rows[k]
                    shifted = val[s, pl.ds(EDGE + r + m - reach, rt), cols]
                    mixing = mixing + row * shifted
                    product_sum = mine * shifted
                    for q in range(0, rt, 8):
                        tap_sums[k] = tap_sums[k] + product_sum[q : q + 8]
                    spread = spread + row * gmix[s, pl.ds(8 + r + reach - m, rt), :]
                strand_out = mixing * (lin * sig)
                if s == 0:
                    outs[pl.ds(r, rt), cols] = strand_out
                else:
                    routs[pl.ds(r, rt), cols] = strand_out.astype(BF16)
                grad = up * mixing * sig * (1.0 + lin * (1.0 - sig)) + spread
                gv[i // (cw // ew), pl.ds(s * rows + r, rt), inner] = grad.astype(BF16)
        tap_sums = [jnp.sum(value, axis=0, keepdims=True) for value in tap_sums]
        small_cols = pl.ds(pl.multiple_of((i % (units // 2 // ew)) * ew, ew), ew)
        pad = [jnp.zeros((1, ew), F32)] * (8 - taps)
        small[i // (units // 2 // ew), pl.ds(0, 8), small_cols] = jnp.concatenate(tap_sums + pad, axis=0)
        return carry

    def elementwise(j):
        if j == 0:
            arrived_x(0)
        if j + 1 < CHUNKS:
            arrived_x(j + 1)
        arrived_y(j)
        for copy in (own[j], over_core[j], over_core2[j]):
            copy.wait_recv()
        projected = jnp.zeros((2 * total, cw), F32)
        for block in range(wg.shape[1]):
            columns = sx[:, :, pl.ds(block * depth, depth)].reshape(2 * total, depth)
            projected = projected + jnp.dot(columns, wg[j, block], preferred_element_type=F32)
        val[:, :, pl.ds(j * cw, cw)] = projected.reshape(2, total, cw)
        lax.fori_loop(j * (cw // ew), (j + 1) * (cw // ew), strand_tile, 0)
        grad_copy(j).start()

    def grad_copy(j):
        return remote(gv.at[j], gvp.at[j], r_ss.at[j, 1], r_rs.at[j, 1], x_id)

    def core_copy(j):
        return remote(core_send.at[j], core_recv.at[j], r_ss.at[j, 0], r_rs.at[j, 0], core_id)

    def product(j):
        grad_copy(j).wait_recv()
        if j == 0:
            stream_copy.wait_recv()
        for side in range(2):
            block = 1 - ci if side == 0 else ci
            mine = pl.ds(pl.multiple_of((2 * xi + block) * depth, depth), depth)
            theirs = pl.ds(pl.multiple_of(block * depth, depth), depth)
            result = jnp.dot(s2t[mine, :], gv[j], preferred_element_type=F32)
            result = result + jnp.dot(s2tp[theirs, :], gvp[j], preferred_element_type=F32)
            if side == 0:
                core_send[j] = result.astype(BF16)
                core_copy(j).start()
            else:
                acc[j] = result

    def after_core(j):
        core_copy(j).wait_recv()
        acc[j] += core_recv[j].astype(F32)
        rs_start(j, 0)

    bases = [0]
    for n, (_, size, split) in enumerate(levels):
        bases.append(bases[-1] + digit(n, 0) * size if split else bases[-1])

    def rows_at(n, d):
        size, split = levels[n][1:]
        base = bases[n] + digit(n, d) * size if split else bases[n]
        return pl.ds(pl.multiple_of(base, 16), size)

    slots, at = {}, 0
    for n, d in exchanges:
        slots[n, d] = at
        at += levels[n][1]
    number = {pair: k for k, pair in enumerate(exchanges)}
    ways = [[d for m, d in exchanges if m == n] for n in range(len(levels))]

    def rs_copy(j, n, d):
        where = pl.ds(slots[n, d], levels[n][1])
        sem = 2 + number[n, d]
        return remote(seq_send.at[j, where], seq_recv.at[j, where], r_ss.at[j, sem], r_rs.at[j, sem], peer_id(n, d))

    def rs_start(j, n):
        for d in ways[n]:
            seq_send[j, pl.ds(slots[n, d], levels[n][1]), :] = acc[j, rows_at(n, d), :].astype(BF16)
            rs_copy(j, n, d).start()

    def rs_finish(j, n):
        for d in ways[n]:
            rs_copy(j, n, d).wait_recv()
        total_rows = acc[j, rows_at(n, 0), :]
        for d in ways[n]:
            total_rows = total_rows + seq_recv[j, pl.ds(slots[n, d], levels[n][1]), :].astype(F32)
        acc[j, rows_at(n, 0), :] = total_rows

    gathers = [n for n in reversed(range(len(levels))) if levels[n][2]]

    def ag_copy(j, n, d):
        size = levels[n][1]
        ref = gathered.at[j, pl.ds(pl.multiple_of(bases[n + 1], 16), size)]
        sem = 2 + len(exchanges) + number[n, d]
        return remote(ref, ref, r_ss.at[j, sem], r_rs.at[j, sem], peer_id(n, d))

    def ag_start(j, n):
        for d in ways[n]:
            ag_copy(j, n, d).start()

    def stages(j):
        def after_rs(n):
            rs_finish(j, n)
            if n + 1 < len(levels):
                rs_start(j, n + 1)
            else:
                last = rows_at(n, 0)
                gathered[j, last, :] = acc[j, last, :].astype(BF16)
                ag_start(j, gathers[0])

        def after_ag(k):
            for d in ways[gathers[k]]:
                ag_copy(j, gathers[k], d).wait_recv()
            if k + 1 < len(gathers):
                ag_start(j, gathers[k + 1])
            else:
                gw_ref[:, pl.ds(j * cw, cw)] = gathered[j]

        steps = [functools.partial(stage, j) for stage in (product, after_core)]
        steps += [functools.partial(after_rs, b) for b in range(len(levels))]
        steps += [functools.partial(after_ag, n) for n in range(len(gathers))]
        return steps

    def back_tile(i, carry):
        b = i // (depth // tile)
        r = pl.ds(pl.multiple_of((i % (depth // tile)) * tile, tile), tile)
        cols = pl.ds(pl.multiple_of(i * tile, tile), tile)
        mirror = pl.ds(pl.multiple_of(width - tile - i * tile, tile), tile)
        part = jnp.zeros((2 * rows, tile), F32)
        for j in range(CHUNKS):
            part = part + lax.dot_general(
                gv[j], wg[j, b, r, :], (((1,), (1,)), ((), ())), preferred_element_type=F32
            )
        fwd_back[:, cols] = part[:rows]
        rev_back[:, mirror] = mirrored(part[rows:].astype(BF16))
        return carry

    one_hot = (
        lax.broadcasted_iota(jnp.int32, (8, rows), 0) == tok_ref[...]
    ).astype(F32).astype(BF16)

    def input_tile(i, carry):
        cols = pl.ds(pl.multiple_of(i * tile, tile), tile)
        grad = fwd_back[:, cols] + rev_back[:, cols]
        top = grad.astype(BF16)
        hout_ref[:, cols] = top
        left = grad - top.astype(F32)
        mid = left.astype(BF16)
        low = (left - mid.astype(F32)).astype(BF16)
        table = jnp.dot(one_hot, top, preferred_element_type=F32)
        table = table + jnp.dot(one_hot, mid, preferred_element_type=F32)
        table = table + jnp.dot(one_hot, low, preferred_element_type=F32)
        per = units // 2 // tile
        where = pl.ds(pl.multiple_of((i % per) * tile, tile), tile)
        at_rows = pl.ds(pl.multiple_of(8 + 8 * ((i // per) % 2), 8), 8)
        small[i // (2 * per), at_rows, where] = table
        return carry


    small_ids = [core_id, x_id] + bit_ids

    def small_copy(n):
        src = small.at[1 - ci] if n == 0 else small.at[2 + (n - 1) % 2]
        return remote(src, small_recv.at[n], s_ss.at[n], s_rs.at[n], small_ids[n])

    def small_last():
        return remote(small_ref.at[ci], small_ref.at[ci], s_ss.at[bits + 2], s_rs.at[bits + 2], core_id)

    def small_step(n):
        small_copy(n).wait_recv()
        base = small[ci] if n == 0 else small[2 + (n - 1) % 2]
        now = base + small_recv[n]
        if n < bits + 1:
            if n >= 2:
                small_copy(n - 1).wait_send()
            small[2 + n % 2] = now
            small_copy(n + 1).start()
        else:
            small_ref[ci] = now
            small_last().start()

    def result_tile(i, carry):
        cols = pl.ds(pl.multiple_of(i * tile, tile), tile)
        mirror = pl.ds(pl.multiple_of(units - tile - i * tile, tile), tile)
        block_ref[:, cols] = (outs[:, cols] + mirrored(routs[:, mirror])).astype(BF16)
        return carry

    tiles = width // tile

    def fill_back(part):
        lax.fori_loop(part * tiles // 4, (part + 1) * tiles // 4, back_tile, 0)

    def fill_input():
        lax.fori_loop(0, tiles, input_tile, 0)
        small_copy(0).start()

    def fill_result():
        lax.fori_loop(0, units // tile, result_tile, 0)
        small_step(0)

    for j in range(CHUNKS):
        elementwise(j)
    for part in range(4):
        fill_back(part)
    fillers = [fill_input, fill_result] + [functools.partial(small_step, n) for n in range(1, bits + 2)]
    plans = [stages(j) for j in range(CHUNKS)]
    length = len(plans[0])
    for wave in range(length + CHUNKS - 1):
        for j in range(CHUNKS):
            if 0 <= wave - j < length:
                plans[j][wave - j]()
        if fillers:
            fillers.pop(0)()
    for filler in fillers:
        filler()
    small_last().wait_recv()
    for h in range(2):
        kernel_ref[:, pl.ds(h * units // 2, units // 2)] = small_ref[h, :taps, :] * factor
        for q in range(2):
            columns = pl.ds((2 * h + q) * (units // 2), units // 2)
            table_ref[:, columns] = small_ref[h, 8 + 8 * q : 8 + 8 * q + vocab, :] * factor

    for copy in sends:
        copy.wait_send()
    for j in range(CHUNKS):
        core_copy(j).wait_send()
        grad_copy(j).wait_send()
        for n, d in exchanges:
            rs_copy(j, n, d).wait_send()
            if levels[n][2]:
                ag_copy(j, n, d).wait_send()
    small_copy(0).wait_send()
    small_copy(bits).wait_send()
    small_copy(bits + 1).wait_send()
    small_last().wait_send()


def finish(factor, b_in, h_in, g_in, k_in, t_in, b_out, h_out, g_out, k_out, t_out, b_mid, h_mid, k_mid, t_mid, narrow, wide, sems):
    step = g_in.shape[0] // 4
    parts = [pl.ds(q * step, step) for q in range(4)]
    inward = [(g_in.at[part], narrow.at[part]) for part in parts]
    inward += [(h_in, h_mid), (b_in, b_mid), (t_in, t_mid), (k_in, k_mid)]
    outward = [(wide.at[part], g_out.at[part]) for part in parts]
    outward += [(h_mid, h_out), (b_mid, b_out), (t_mid, t_out), (k_mid, k_out)]
    fetches = [pltpu.make_async_copy(src, dst, sems.at[n]) for n, (src, dst) in enumerate(inward)]
    stores = [pltpu.make_async_copy(src, dst, sems.at[8 + n]) for n, (src, dst) in enumerate(outward)]
    for copy in fetches:
        copy.start()
    for n in range(8):
        fetches[n].wait()
        if n < 4:
            wide[parts[n], :] = narrow[parts[n], :].astype(F32) * factor
        stores[n].start()
    for copy in stores:
        copy.wait()


def local(seq_count, hidden, tokens, embedding, weight, kernel, cotangent):
    window, token_codes, upstream = hidden[0], tokens[0], cotangent[0]
    rows, width = window.shape
    depth, units = weight.shape
    blocks = width // depth
    taps, vocab = kernel.shape[0], embedding.shape[0]
    bits = seq_count.bit_length() - 1
    positions = hidden.shape[0] * rows * lax.axis_size("dp") * seq_count
    total = rows + 2 * EDGE
    cw = units // CHUNKS
    factor = 1.0 / math.sqrt(positions)
    levels = level_plan(depth, bits)
    stacked_rows = sum(size * ((1 << len(group)) - 1) for group, size, _ in levels)
    copies = sum((1 << len(group)) - 1 for group, _, _ in levels)
    vmem = pl.BlockSpec(memory_space=pltpu.VMEM)
    dma = pltpu.SemaphoreType.DMA
    block_result, grad_hidden, grad_weight, kernel_sum, table = pl.pallas_call(
        functools.partial(body, seq_count, bits, factor),
        out_shape=(
            jax.ShapeDtypeStruct((rows, units), BF16),
            jax.ShapeDtypeStruct((rows, width), BF16),
            jax.ShapeDtypeStruct((depth, units), BF16),
            jax.ShapeDtypeStruct((taps, units), F32),
            jax.ShapeDtypeStruct((vocab, width), F32),
        ),
        in_specs=[pl.BlockSpec(memory_space=pltpu.HBM)] * 6,
        out_specs=(vmem,) * 5,
        scratch_shapes=[
            pltpu.VMEM((rows, width), BF16),
            pltpu.VMEM((1, rows), jnp.int32),
            pltpu.VMEM((vocab, width), F32),
            pltpu.VMEM((taps, units), F32),
            pltpu.VMEM((rows, units), BF16),
            pltpu.VMEM((CHUNKS, blocks, depth, cw), BF16),
            pltpu.VMEM((2, total, width), BF16),
            pltpu.VMEM((2, EDGE, width), BF16),
            pltpu.VMEM((2, total, units), BF16),
            pltpu.VMEM((2, EDGE, units), BF16),
            pltpu.VMEM((width, 2 * rows), BF16),
            pltpu.VMEM((2 * depth, 2 * rows), BF16),
            pltpu.VMEM((2, total, units), F32),
            pltpu.VMEM((2, rows + 16, 128), F32),
            pltpu.VMEM((2, rows + 16, 128), F32),
            pltpu.VMEM((rows, units), F32),
            pltpu.VMEM((rows, units), BF16),
            pltpu.VMEM((CHUNKS, 2 * rows, cw), BF16),
            pltpu.VMEM((CHUNKS, 2 * rows, cw), BF16),
            pltpu.VMEM((rows, width), F32),
            pltpu.VMEM((rows, width), F32),
            pltpu.VMEM((CHUNKS, depth, cw), F32),
            pltpu.VMEM((CHUNKS, depth, cw), BF16),
            pltpu.VMEM((CHUNKS, depth, cw), BF16),
            pltpu.VMEM((CHUNKS, stacked_rows, cw), BF16),
            pltpu.VMEM((CHUNKS, stacked_rows, cw), BF16),
            pltpu.VMEM((CHUNKS, depth, cw), BF16),
            pltpu.VMEM((4, 24, units // 2), F32),
            pltpu.VMEM((bits + 2, 24, units // 2), F32),
            pltpu.VMEM((2, 24, units // 2), F32),
            dma((5 + CHUNKS,)),
            dma((5 * CHUNKS,)), dma((5 * CHUNKS,)),
            dma((5,)), dma((5,)),
            dma((CHUNKS, 2 + 2 * copies)), dma((CHUNKS, 2 + 2 * copies)),
            dma((bits + 3,)), dma((bits + 3,)),
        ],
        compiler_params=pltpu.CompilerParams(
            collective_id=0, has_side_effects=True, vmem_limit_bytes=60 * 1024 * 1024
        ),
        cost_estimate=pl.CostEstimate(
            flops=12 * rows * width * units, bytes_accessed=8 * rows * width, transcendentals=4 * rows * units
        ),
    )(
        window,
        token_codes.reshape(1, rows),
        embedding,
        weight,
        kernel,
        upstream,
    )
    block_result, grad_hidden, grad_weight, kernel_sum, table = pl.pallas_call(
        functools.partial(finish, factor),
        out_shape=(
            jax.ShapeDtypeStruct((rows, units), BF16),
            jax.ShapeDtypeStruct((rows, width), BF16),
            jax.ShapeDtypeStruct((depth, units), F32),
            jax.ShapeDtypeStruct((taps, units), F32),
            jax.ShapeDtypeStruct((vocab, width), F32),
        ),
        in_specs=[pl.BlockSpec(memory_space=pltpu.HBM)] * 5,
        out_specs=(pl.BlockSpec(memory_space=pltpu.HBM),) * 5,
        scratch_shapes=[
            pltpu.VMEM((rows, units), BF16),
            pltpu.VMEM((rows, width), BF16),
            pltpu.VMEM((taps, units), F32),
            pltpu.VMEM((vocab, width), F32),
            pltpu.VMEM((depth, units), BF16),
            pltpu.VMEM((depth, units), F32),
            dma((16,)),
        ],
        compiler_params=pltpu.CompilerParams(vmem_limit_bytes=60 * 1024 * 1024),
    )(block_result, grad_hidden, grad_weight, kernel_sum, table)
    return (
        block_result[None],
        grad_hidden[None],
        grad_weight,
        kernel_sum,
        table,
    )


def solution(mesh):
    in_specs = (P("dp", "seq", None), P("dp", "seq"), P(), P("dp", None), P(), P("dp", "seq", None))
    out_specs = (P("dp", "seq", None), P("dp", "seq", None), P("dp", None), P(), P())
    return jax.shard_map(
        functools.partial(local, mesh.shape["seq"]),
        mesh=mesh, in_specs=in_specs, out_specs=out_specs, check_vma=False,
    )
```

```python
import functools
import math

import jax
import jax.numpy as jnp
from jax import lax
from jax.experimental import pallas as pl
from jax.experimental.pallas import tpu as pltpu
from jax.sharding import PartitionSpec as P

MESH = pl.DeviceIdType.MESH
F32 = jnp.float32
BF16 = jnp.bfloat16
EDGE = 16
CHUNKS = 4
LANES = 256


def level_plan(rows, bits):
    groups = [[0], [1, 2]] + [[b] for b in range(3, bits)] if bits >= 3 else [[b] for b in range(bits)]
    levels = []
    for group in groups:
        ways = 1 << len(group)
        split = rows % (16 * ways) == 0
        if split:
            rows //= ways
            levels.append((group, rows, True))
        else:
            levels += [([b], rows, False) for b in group]
    return levels


def body(
    seq_count, bits, factor,
    hid_in, tok_in, emb_in, w_in, ker_in, cot_in,
    block_ref, hout_ref, gw_ref, kernel_ref, table_ref,
    hid_ref, tok_ref, emb_ref, ker_ref, cot_ref,
    wg, sx, hx, ux, hu, s2t, s2tp, val, gmix, sigs, outs, routs, gv, gvp, fwd_back, rev_back,
    acc, core_send, core_recv, seq_send, seq_recv, gathered,
    small, small_recv, small_ref,
    in_sems, w_ss, w_rs, h_ss, h_rs, r_ss, r_rs, s_ss, s_rs,
):
    rows = hid_ref.shape[0]
    depth, units = w_in.shape
    width = hid_ref.shape[1]
    taps = ker_ref.shape[0]
    reach = (taps - 1) // 2
    vocab = emb_ref.shape[0]
    total = rows + 2 * EDGE
    dp = lax.axis_index("dp")
    seq = lax.axis_index("seq")
    xi, ci = dp // 2, dp % 2
    cw = units // CHUNKS
    w_loads = [
        pltpu.make_async_copy(w_in.at[:, pl.ds(p * cw, cw)], wg.at[p, dp], in_sems.at[5 + p]) for p in range(CHUNKS)
    ]
    loads = [
        pltpu.make_async_copy(src, dst, in_sems.at[n])
        for n, (src, dst) in enumerate(
            [(cot_in, cot_ref), (hid_in, hid_ref), (tok_in, tok_ref), (emb_in, emb_ref), (ker_in, ker_ref)]
        )
    ]
    for copy in w_loads + loads:
        copy.start()
    core_id = (dp + 1 - 2 * ci, seq)
    x_id = (dp + 2 - 4 * xi, seq)
    bit_vals = [(seq // (1 << b)) % 2 for b in range(bits)]
    bit_ids = [(dp, seq + (1 - 2 * bit_vals[b]) * (1 << b)) for b in range(bits)]
    left_id = (dp, (seq + seq_count - 1) % seq_count)
    right_id = (dp, (seq + 1) % seq_count)

    levels = level_plan(depth, bits)
    exchanges = [(n, d) for n, (group, _, _) in enumerate(levels) for d in range(1, 1 << len(group))]

    def peer_id(n, d):
        place = seq
        for at_bit, b in enumerate(levels[n][0]):
            if (d >> at_bit) & 1:
                place = place + (1 - 2 * bit_vals[b]) * (1 << b)
        return (dp, place)

    def digit(n, d):
        value = 0
        for at_bit, b in enumerate(levels[n][0]):
            bit = bit_vals[b]
            value = value + (1 - bit if (d >> at_bit) & 1 else bit) * (1 << at_bit)
        return value

    partners = [core_id, x_id] + [peer_id(n, d) for n, d in exchanges] + [left_id, right_id]
    barrier = pltpu.get_barrier_semaphore()
    for partner in partners:
        pl.semaphore_signal(barrier, inc=1, device_id=partner, device_id_type=MESH)
    pl.semaphore_wait(barrier, len(partners))

    def remote(src, dst, ss, rs, who):
        return pltpu.make_async_remote_copy(
            src_ref=src, dst_ref=dst, send_sem=ss, recv_sem=rs, device_id=who, device_id_type=MESH
        )

    yi = bit_vals[0]
    y_id = bit_ids[0]
    dpx = dp + 2 - 4 * xi
    half = depth // 2

    def part_of(p, block, side):
        return wg.at[p, block, pl.ds(pl.multiple_of(side * half, 16), half)]

    def passed(p, block, side, sem, who):
        part = wg.at[p, block] if side is None else part_of(p, block, side)
        return remote(part, part, w_ss.at[sem * CHUNKS + p], w_rs.at[sem * CHUNKS + p], who)

    over_x = lambda p: passed(p, dp, yi, 0, x_id)
    own = lambda p: passed(p, dp, None, 1, core_id)
    over_y = lambda p: passed(p, dpx, yi, 2, y_id)
    over_core = lambda p: passed(p, dpx, yi, 3, core_id)
    over_core2 = lambda p: passed(p, dpx, 1 - yi, 4, core_id)
    for p in range(CHUNKS):
        w_loads[p].wait()
        over_x(p).start()
        own(p).start()
    loads[0].wait()
    sends = []
    halo_u = [
        remote(cot_ref.at[pl.ds(rows - EDGE, EDGE)], hu.at[0], h_ss.at[0], h_rs.at[0], right_id),
        remote(cot_ref.at[pl.ds(0, EDGE)], hu.at[1], h_ss.at[1], h_rs.at[1], left_id),
    ]
    for copy in halo_u:
        copy.start()

    tile = LANES
    for copy in loads[1:]:
        copy.wait()
    tok = jnp.broadcast_to(tok_ref[...], (rows, rows)).astype(F32).T
    tok = jnp.concatenate([tok] * (tile // rows), axis=1) if tile > rows else tok[:, :tile]

    def stream_tile(i, carry):
        cols = pl.ds(pl.multiple_of(i * tile, tile), tile)
        looked = jnp.zeros((rows, tile), F32)
        for k in range(vocab):
            looked = looked + jnp.where(tok == float(k), emb_ref[pl.ds(k, 1), cols], 0.0)
        sx[0, pl.ds(EDGE, rows), cols] = (hid_ref[:, cols].astype(F32) + looked).astype(BF16)
        return carry

    lax.fori_loop(0, width // tile, stream_tile, 0)
    halo_s = [
        remote(sx.at[0, pl.ds(rows, EDGE)], hx.at[0], h_ss.at[2], h_rs.at[2], right_id),
        remote(sx.at[0, pl.ds(EDGE, EDGE)], hx.at[1], h_ss.at[3], h_rs.at[3], left_id),
    ]
    for copy in halo_s:
        copy.start()
    sends += halo_u + halo_s

    has_left = (seq > 0).astype(F32)
    has_right = (seq < seq_count - 1).astype(F32)
    ux[0, pl.ds(EDGE, rows), :] = cot_ref[...]
    for copy in halo_u + halo_s:
        copy.wait_recv()
    sx[0, pl.ds(0, EDGE), :] = (hx[0].astype(F32) * has_left).astype(BF16)
    sx[0, pl.ds(rows + EDGE, EDGE), :] = (hx[1].astype(F32) * has_right).astype(BF16)
    ux[0, pl.ds(0, EDGE), :] = (hu[0].astype(F32) * has_left).astype(BF16)
    ux[0, pl.ds(rows + EDGE, EDGE), :] = (hu[1].astype(F32) * has_right).astype(BF16)

    flip = (
        lax.broadcasted_iota(jnp.int32, (tile, tile), 0)
        + lax.broadcasted_iota(jnp.int32, (tile, tile), 1)
        == tile - 1
    ).astype(F32).astype(BF16)

    def mirrored(block):
        return jnp.dot(block, flip, preferred_element_type=F32)

    def reverse_stream(i, carry):
        cols = pl.ds(pl.multiple_of(i * tile, tile), tile)
        back = pl.ds(pl.multiple_of(width - tile - i * tile, tile), tile)
        sx[1, :, back] = mirrored(sx[0, :, cols]).astype(BF16)
        return carry

    lax.fori_loop(0, width // tile, reverse_stream, 0)

    def reverse_up(i, carry):
        cols = pl.ds(pl.multiple_of(i * tile, tile), tile)
        back = pl.ds(pl.multiple_of(units - tile - i * tile, tile), tile)
        ux[1, :, back] = mirrored(ux[0, :, cols]).astype(BF16)
        return carry

    lax.fori_loop(0, units // tile, reverse_up, 0)

    def arrived_x(p):
        over_x(p).wait_recv()
        over_y(p).start()
        over_core(p).start()

    def arrived_y(p):
        over_y(p).wait_recv()
        over_core2(p).start()

    def transpose_tile(i, carry):
        cols = pl.ds(pl.multiple_of(i * tile, tile), tile)
        for s in range(2):
            s2t[cols, pl.ds(s * rows, rows)] = sx[s, pl.ds(EDGE, rows), cols].T
        return carry

    lax.fori_loop(0, width // tile, transpose_tile, 0)
    stream_copy = remote(
        s2t.at[pl.ds(pl.multiple_of((1 - xi) * 2 * depth, depth), 2 * depth)], s2tp, h_ss.at[4], h_rs.at[4], x_id
    )
    sends.append(stream_copy)

    ew = 128
    lo = EDGE - 8

    rt = 32

    def strand_tile(i, carry):
        cols = pl.ds(pl.multiple_of(i * ew, ew), ew)
        inner = pl.ds(pl.multiple_of((i % (cw // ew)) * ew, ew), ew)
        tap_rows = [ker_ref[pl.ds(k, 1), cols] for k in range(taps)]
        tap_sums = [jnp.zeros((8, ew), F32)] * taps
        for s in range(2):
            for r in range(0, rows + 16, rt // 2):
                at = pl.ds(lo + r, rt // 2)
                part = val[s, at, cols].astype(BF16).astype(F32)
                val[s, at, cols] = part
                logistic = jax.nn.sigmoid(part)
                gate = part * logistic
                sigs[s, pl.ds(r, rt // 2), :] = logistic
                gmix[s, pl.ds(r, rt // 2), :] = ux[s, at, cols].astype(F32) * gate
            for r in range(0, rows, rt):
                lin = val[s, pl.ds(EDGE + r, rt), cols]
                sig = sigs[s, pl.ds(8 + r, rt), :]
                up = ux[s, pl.ds(EDGE + r, rt), cols].astype(F32)
                mine = gmix[s, pl.ds(8 + r, rt), :]
                mixing = jnp.zeros((rt, ew), F32)
                spread = jnp.zeros((rt, ew), F32)
                for m in range(taps):
                    k = m if s == 0 else taps - 1 - m
                    row = tap_rows[k]
                    shifted = val[s, pl.ds(EDGE + r + m - reach, rt), cols]
                    mixing = mixing + row * shifted
                    product_sum = mine * shifted
                    for q in range(0, rt, 8):
                        tap_sums[k] = tap_sums[k] + product_sum[q : q + 8]
                    spread = spread + row * gmix[s, pl.ds(8 + r + reach - m, rt), :]
                strand_out = mixing * (lin * sig)
                if s == 0:
                    outs[pl.ds(r, rt), cols] = strand_out
                else:
                    routs[pl.ds(r, rt), cols] = strand_out.astype(BF16)
                grad = up * mixing * sig * (1.0 + lin * (1.0 - sig)) + spread
                gv[i // (cw // ew), pl.ds(s * rows + r, rt), inner] = grad.astype(BF16)
        tap_sums = [jnp.sum(value, axis=0, keepdims=True) for value in tap_sums]
        small_cols = pl.ds(pl.multiple_of((i % (units // 2 // ew)) * ew, ew), ew)
        pad = [jnp.zeros((1, ew), F32)] * (8 - taps)
        small[i // (units // 2 // ew), pl.ds(0, 8), small_cols] = jnp.concatenate(tap_sums + pad, axis=0)
        return carry

    def elementwise(j):
        @pl.when(j + 1 < CHUNKS)
        def _():
            arrived_x(j + 1)

        @pl.when(j + 2 == CHUNKS)
        def _():
            stream_copy.start()

        arrived_y(j)
        for copy in (own(j), over_core(j), over_core2(j)):
            copy.wait_recv()
        projected = jnp.zeros((2 * total, cw), F32)
        for block in range(wg.shape[1]):
            columns = sx[:, :, pl.ds(block * depth, depth)].reshape(2 * total, depth)
            projected = projected + jnp.dot(columns, wg[j, block], preferred_element_type=F32)
        val[:, :, pl.ds(pl.multiple_of(j * cw, cw), cw)] = projected.reshape(2, total, cw)
        lax.fori_loop(0, cw // ew, lambda q, carry: strand_tile(j * (cw // ew) + q, carry), 0)
        grad_copy(j).start()

    def grad_copy(j):
        return remote(gv.at[j], gvp.at[j], r_ss.at[j, 1], r_rs.at[j, 1], x_id)

    def core_copy(j):
        return remote(core_send.at[j], core_recv.at[j], r_ss.at[j, 0], r_rs.at[j, 0], core_id)

    def product(j):
        @pl.when(j == 0)
        def _():
            stream_copy.wait_recv()

        grad_copy(j).wait_recv()
        for side in range(2):
            block = 1 - ci if side == 0 else ci
            mine = pl.ds(pl.multiple_of((2 * xi + block) * depth, depth), depth)
            theirs = pl.ds(pl.multiple_of(block * depth, depth), depth)
            result = jnp.dot(s2t[mine, :], gv[j], preferred_element_type=F32)
            result = result + jnp.dot(s2tp[theirs, :], gvp[j], preferred_element_type=F32)
            if side == 0:
                core_send[j] = result.astype(BF16)
                core_copy(j).start()
            else:
                acc[j] = result

    def after_core(j):
        core_copy(j).wait_recv()
        acc[j] += core_recv[j].astype(F32)
        rs_start(j, 0)

    bases = [0]
    for n, (_, size, split) in enumerate(levels):
        bases.append(bases[-1] + digit(n, 0) * size if split else bases[-1])

    def rows_at(n, d):
        size, split = levels[n][1:]
        base = bases[n] + digit(n, d) * size if split else bases[n]
        return pl.ds(pl.multiple_of(base, 16), size)

    slots, at = {}, 0
    for n, d in exchanges:
        slots[n, d] = at
        at += levels[n][1]
    number = {pair: k for k, pair in enumerate(exchanges)}
    ways = [[d for m, d in exchanges if m == n] for n in range(len(levels))]

    def rs_copy(j, n, d):
        where = pl.ds(slots[n, d], levels[n][1])
        sem = 2 + number[n, d]
        return remote(seq_send.at[j, where], seq_recv.at[j, where], r_ss.at[j, sem], r_rs.at[j, sem], peer_id(n, d))

    def rs_start(j, n):
        for d in ways[n]:
            seq_send[j, pl.ds(slots[n, d], levels[n][1]), :] = acc[j, rows_at(n, d), :].astype(BF16)
            rs_copy(j, n, d).start()

    def rs_finish(j, n):
        for d in ways[n]:
            rs_copy(j, n, d).wait_recv()
        total_rows = acc[j, rows_at(n, 0), :]
        for d in ways[n]:
            total_rows = total_rows + seq_recv[j, pl.ds(slots[n, d], levels[n][1]), :].astype(F32)
        acc[j, rows_at(n, 0), :] = total_rows

    gathers = [n for n in reversed(range(len(levels))) if levels[n][2]]

    def ag_copy(j, n, d):
        size = levels[n][1]
        ref = gathered.at[j, pl.ds(pl.multiple_of(bases[n + 1], 16), size)]
        sem = 2 + len(exchanges) + number[n, d]
        return remote(ref, ref, r_ss.at[j, sem], r_rs.at[j, sem], peer_id(n, d))

    def ag_start(j, n):
        for d in ways[n]:
            ag_copy(j, n, d).start()

    def stages(j):
        def after_rs(n):
            rs_finish(j, n)
            if n + 1 < len(levels):
                rs_start(j, n + 1)
            else:
                last = rows_at(n, 0)
                gathered[j, last, :] = acc[j, last, :].astype(BF16)
                ag_start(j, gathers[0])

        def after_ag(k):
            for d in ways[gathers[k]]:
                ag_copy(j, gathers[k], d).wait_recv()
            if k + 1 < len(gathers):
                ag_start(j, gathers[k + 1])
            else:
                gw_ref[:, pl.ds(pl.multiple_of(j * cw, cw), cw)] = gathered[j]

        steps = [functools.partial(stage, j) for stage in (product, after_core)]
        steps += [functools.partial(after_rs, b) for b in range(len(levels))]
        steps += [functools.partial(after_ag, n) for n in range(len(gathers))]
        return steps

    def back_tile(i, carry):
        b = i // (depth // tile)
        r = pl.ds(pl.multiple_of((i % (depth // tile)) * tile, tile), tile)
        cols = pl.ds(pl.multiple_of(i * tile, tile), tile)
        mirror = pl.ds(pl.multiple_of(width - tile - i * tile, tile), tile)
        part = jnp.zeros((2 * rows, tile), F32)
        for j in range(CHUNKS):
            part = part + lax.dot_general(
                gv[j], wg[j, b, r, :], (((1,), (1,)), ((), ())), preferred_element_type=F32
            )
        fwd_back[:, cols] = part[:rows]
        rev_back[:, mirror] = mirrored(part[rows:].astype(BF16))
        return carry

    one_hot = (
        lax.broadcasted_iota(jnp.int32, (8, rows), 0) == tok_ref[...]
    ).astype(F32).astype(BF16)

    def input_tile(i, carry):
        cols = pl.ds(pl.multiple_of(i * tile, tile), tile)
        grad = fwd_back[:, cols] + rev_back[:, cols]
        top = grad.astype(BF16)
        hout_ref[:, cols] = top
        left = grad - top.astype(F32)
        mid = left.astype(BF16)
        low = (left - mid.astype(F32)).astype(BF16)
        table = jnp.dot(one_hot, top, preferred_element_type=F32)
        table = table + jnp.dot(one_hot, mid, preferred_element_type=F32)
        table = table + jnp.dot(one_hot, low, preferred_element_type=F32)
        per = units // 2 // tile
        where = pl.ds(pl.multiple_of((i % per) * tile, tile), tile)
        at_rows = pl.ds(pl.multiple_of(8 + 8 * ((i // per) % 2), 8), 8)
        small[i // (2 * per), at_rows, where] = table
        return carry


    small_ids = [core_id, x_id] + bit_ids

    def small_copy(n):
        src = small.at[1 - ci] if n == 0 else small.at[2 + (n - 1) % 2]
        return remote(src, small_recv.at[n], s_ss.at[n], s_rs.at[n], small_ids[n])

    def small_last():
        return remote(small_ref.at[ci], small_ref.at[ci], s_ss.at[bits + 2], s_rs.at[bits + 2], core_id)

    def small_step(n):
        small_copy(n).wait_recv()
        base = small[ci] if n == 0 else small[2 + (n - 1) % 2]
        now = base + small_recv[n]
        if n < bits + 1:
            if n >= 2:
                small_copy(n - 1).wait_send()
            small[2 + n % 2] = now
            small_copy(n + 1).start()
        else:
            small_ref[ci] = now
            small_last().start()

    def result_tile(i, carry):
        cols = pl.ds(pl.multiple_of(i * tile, tile), tile)
        mirror = pl.ds(pl.multiple_of(units - tile - i * tile, tile), tile)
        block_ref[:, cols] = (outs[:, cols] + mirrored(routs[:, mirror])).astype(BF16)
        return carry

    tiles = width // tile

    def fill_input():
        lax.fori_loop(0, tiles, input_tile, 0)
        small_copy(0).start()

    def fill_result():
        lax.fori_loop(0, units // tile, result_tile, 0)
        small_step(0)

    arrived_x(0)

    def elementwise_step(j, carry):
        elementwise(j)
        return carry

    lax.fori_loop(0, CHUNKS, elementwise_step, 0)
    lax.fori_loop(0, tiles, back_tile, 0)

    fillers = [fill_input, fill_result] + [functools.partial(small_step, n) for n in range(1, bits + 2)]
    length = len(stages(0))
    waves = length + CHUNKS - 1

    def wave_step(wave, carry):
        for at_stage in reversed(range(length)):
            j = wave - at_stage

            @pl.when((j >= 0) & (j < CHUNKS))
            def _():
                stages(j)[at_stage]()

        for n, filler in enumerate(fillers[:waves]):
            pl.when(wave == n)(filler)
        return carry

    lax.fori_loop(0, waves, wave_step, 0)
    for filler in fillers[waves:]:
        filler()
    small_last().wait_recv()
    for h in range(2):
        kernel_ref[:, pl.ds(h * units // 2, units // 2)] = small_ref[h, :taps, :] * factor
        for q in range(2):
            columns = pl.ds((2 * h + q) * (units // 2), units // 2)
            table_ref[:, columns] = small_ref[h, 8 + 8 * q : 8 + 8 * q + vocab, :] * factor

    for copy in sends:
        copy.wait_send()

    def drain(j, carry):
        for copy in (over_x(j), own(j), over_y(j), over_core(j), over_core2(j), core_copy(j), grad_copy(j)):
            copy.wait_send()
        for n, d in exchanges:
            rs_copy(j, n, d).wait_send()
            if levels[n][2]:
                ag_copy(j, n, d).wait_send()
        return carry

    lax.fori_loop(0, CHUNKS, drain, 0)
    small_copy(0).wait_send()
    small_copy(bits).wait_send()
    small_copy(bits + 1).wait_send()
    small_last().wait_send()


def finish(factor, b_in, h_in, g_in, k_in, t_in, b_out, h_out, g_out, k_out, t_out, b_mid, h_mid, k_mid, t_mid, narrow, wide, sems):
    step = g_in.shape[0] // 4
    parts = [pl.ds(q * step, step) for q in range(4)]
    inward = [(g_in.at[part], narrow.at[part]) for part in parts]
    inward += [(h_in, h_mid), (b_in, b_mid), (t_in, t_mid), (k_in, k_mid)]
    outward = [(wide.at[part], g_out.at[part]) for part in parts]
    outward += [(h_mid, h_out), (b_mid, b_out), (t_mid, t_out), (k_mid, k_out)]
    fetches = [pltpu.make_async_copy(src, dst, sems.at[n]) for n, (src, dst) in enumerate(inward)]
    stores = [pltpu.make_async_copy(src, dst, sems.at[8 + n]) for n, (src, dst) in enumerate(outward)]
    for copy in fetches:
        copy.start()
    for n in range(8):
        fetches[n].wait()
        if n < 4:
            wide[parts[n], :] = narrow[parts[n], :].astype(F32) * factor
        stores[n].start()
    for copy in stores:
        copy.wait()


def local(seq_count, hidden, tokens, embedding, weight, kernel, cotangent):
    window, token_codes, upstream = hidden[0], tokens[0], cotangent[0]
    rows, width = window.shape
    depth, units = weight.shape
    blocks = width // depth
    taps, vocab = kernel.shape[0], embedding.shape[0]
    bits = seq_count.bit_length() - 1
    positions = hidden.shape[0] * rows * lax.axis_size("dp") * seq_count
    total = rows + 2 * EDGE
    cw = units // CHUNKS
    factor = 1.0 / math.sqrt(positions)
    levels = level_plan(depth, bits)
    stacked_rows = sum(size * ((1 << len(group)) - 1) for group, size, _ in levels)
    copies = sum((1 << len(group)) - 1 for group, _, _ in levels)
    vmem = pl.BlockSpec(memory_space=pltpu.VMEM)
    dma = pltpu.SemaphoreType.DMA
    block_result, grad_hidden, grad_weight, kernel_sum, table = pl.pallas_call(
        functools.partial(body, seq_count, bits, factor),
        out_shape=(
            jax.ShapeDtypeStruct((rows, units), BF16),
            jax.ShapeDtypeStruct((rows, width), BF16),
            jax.ShapeDtypeStruct((depth, units), BF16),
            jax.ShapeDtypeStruct((taps, units), F32),
            jax.ShapeDtypeStruct((vocab, width), F32),
        ),
        in_specs=[pl.BlockSpec(memory_space=pltpu.HBM)] * 6,
        out_specs=(vmem,) * 5,
        scratch_shapes=[
            pltpu.VMEM((rows, width), BF16),
            pltpu.VMEM((1, rows), jnp.int32),
            pltpu.VMEM((vocab, width), F32),
            pltpu.VMEM((taps, units), F32),
            pltpu.VMEM((rows, units), BF16),
            pltpu.VMEM((CHUNKS, blocks, depth, cw), BF16),
            pltpu.VMEM((2, total, width), BF16),
            pltpu.VMEM((2, EDGE, width), BF16),
            pltpu.VMEM((2, total, units), BF16),
            pltpu.VMEM((2, EDGE, units), BF16),
            pltpu.VMEM((width, 2 * rows), BF16),
            pltpu.VMEM((2 * depth, 2 * rows), BF16),
            pltpu.VMEM((2, total, units), F32),
            pltpu.VMEM((2, rows + 16, 128), F32),
            pltpu.VMEM((2, rows + 16, 128), F32),
            pltpu.VMEM((rows, units), F32),
            pltpu.VMEM((rows, units), BF16),
            pltpu.VMEM((CHUNKS, 2 * rows, cw), BF16),
            pltpu.VMEM((CHUNKS, 2 * rows, cw), BF16),
            pltpu.VMEM((rows, width), F32),
            pltpu.VMEM((rows, width), F32),
            pltpu.VMEM((CHUNKS, depth, cw), F32),
            pltpu.VMEM((CHUNKS, depth, cw), BF16),
            pltpu.VMEM((CHUNKS, depth, cw), BF16),
            pltpu.VMEM((CHUNKS, stacked_rows, cw), BF16),
            pltpu.VMEM((CHUNKS, stacked_rows, cw), BF16),
            pltpu.VMEM((CHUNKS, depth, cw), BF16),
            pltpu.VMEM((4, 24, units // 2), F32),
            pltpu.VMEM((bits + 2, 24, units // 2), F32),
            pltpu.VMEM((2, 24, units // 2), F32),
            dma((5 + CHUNKS,)),
            dma((5 * CHUNKS,)), dma((5 * CHUNKS,)),
            dma((5,)), dma((5,)),
            dma((CHUNKS, 2 + 2 * copies)), dma((CHUNKS, 2 + 2 * copies)),
            dma((bits + 3,)), dma((bits + 3,)),
        ],
        compiler_params=pltpu.CompilerParams(
            collective_id=0, has_side_effects=True, vmem_limit_bytes=60 * 1024 * 1024
        ),
        cost_estimate=pl.CostEstimate(
            flops=12 * rows * width * units, bytes_accessed=8 * rows * width, transcendentals=4 * rows * units
        ),
    )(
        window,
        token_codes.reshape(1, rows),
        embedding,
        weight,
        kernel,
        upstream,
    )
    block_result, grad_hidden, grad_weight, kernel_sum, table = pl.pallas_call(
        functools.partial(finish, factor),
        out_shape=(
            jax.ShapeDtypeStruct((rows, units), BF16),
            jax.ShapeDtypeStruct((rows, width), BF16),
            jax.ShapeDtypeStruct((depth, units), F32),
            jax.ShapeDtypeStruct((taps, units), F32),
            jax.ShapeDtypeStruct((vocab, width), F32),
        ),
        in_specs=[pl.BlockSpec(memory_space=pltpu.HBM)] * 5,
        out_specs=(pl.BlockSpec(memory_space=pltpu.HBM),) * 5,
        scratch_shapes=[
            pltpu.VMEM((rows, units), BF16),
            pltpu.VMEM((rows, width), BF16),
            pltpu.VMEM((taps, units), F32),
            pltpu.VMEM((vocab, width), F32),
            pltpu.VMEM((depth, units), BF16),
            pltpu.VMEM((depth, units), F32),
            dma((16,)),
        ],
        compiler_params=pltpu.CompilerParams(vmem_limit_bytes=60 * 1024 * 1024),
    )(block_result, grad_hidden, grad_weight, kernel_sum, table)
    return (
        block_result[None],
        grad_hidden[None],
        grad_weight,
        kernel_sum,
        table,
    )


def solution(mesh):
    in_specs = (P("dp", "seq", None), P("dp", "seq"), P(), P("dp", None), P(), P("dp", "seq", None))
    out_specs = (P("dp", "seq", None), P("dp", "seq", None), P("dp", None), P(), P())
    return jax.shard_map(
        functools.partial(local, mesh.shape["seq"]),
        mesh=mesh, in_specs=in_specs, out_specs=out_specs, check_vma=False,
    )
```

```python
import functools
import math

import jax
import jax.numpy as jnp
from jax import lax
from jax.experimental import pallas as pl
from jax.experimental.pallas import tpu as pltpu
from jax.sharding import PartitionSpec as P

MESH = pl.DeviceIdType.MESH
F32 = jnp.float32
BF16 = jnp.bfloat16
EDGE = 16
CHUNKS = 4
LANES = 256


def level_plan(rows, bits):
    groups = [[0], [1, 2]] + [[b] for b in range(3, bits)] if bits >= 3 else [[b] for b in range(bits)]
    levels = []
    for group in groups:
        ways = 1 << len(group)
        split = rows % (16 * ways) == 0
        if split:
            rows //= ways
            levels.append((group, rows, True))
        else:
            levels += [([b], rows, False) for b in group]
    return levels


def body(
    seq_count, bits, factor,
    hid_in, tok_in, emb_in, w_in, ker_in, cot_in,
    block_ref, hout_ref, gw_ref, kernel_ref, table_ref,
    hid_ref, tok_ref, emb_ref, ker_ref, cot_ref,
    wg, sx, hx, ux, hu, s2t, s2tp, val, gmix, sigs, outs, routs, gv, gvp, fwd_back, rev_back,
    acc, core_send, core_recv, seq_send, seq_recv, gathered,
    small, small_recv, small_ref,
    in_sems, w_ss, w_rs, h_ss, h_rs, r_ss, r_rs, s_ss, s_rs,
):
    rows = hid_ref.shape[0]
    depth, units = w_in.shape
    width = hid_ref.shape[1]
    taps = ker_ref.shape[0]
    reach = (taps - 1) // 2
    vocab = emb_ref.shape[0]
    total = rows + 2 * EDGE
    dp = lax.axis_index("dp")
    seq = lax.axis_index("seq")
    xi, ci = dp // 2, dp % 2
    cw = units // CHUNKS
    w_loads = [
        pltpu.make_async_copy(w_in.at[:, pl.ds(p * cw, cw)], wg.at[p, dp], in_sems.at[5 + p]) for p in range(CHUNKS)
    ]
    loads = [
        pltpu.make_async_copy(src, dst, in_sems.at[n])
        for n, (src, dst) in enumerate(
            [(cot_in, cot_ref), (hid_in, hid_ref), (tok_in, tok_ref), (emb_in, emb_ref), (ker_in, ker_ref)]
        )
    ]
    for copy in w_loads + loads:
        copy.start()
    core_id = (dp + 1 - 2 * ci, seq)
    x_id = (dp + 2 - 4 * xi, seq)
    bit_vals = [(seq // (1 << b)) % 2 for b in range(bits)]
    bit_ids = [(dp, seq + (1 - 2 * bit_vals[b]) * (1 << b)) for b in range(bits)]
    left_id = (dp, (seq + seq_count - 1) % seq_count)
    right_id = (dp, (seq + 1) % seq_count)

    levels = level_plan(depth, bits)
    exchanges = [(n, d) for n, (group, _, _) in enumerate(levels) for d in range(1, 1 << len(group))]

    def peer_id(n, d):
        place = seq
        for at_bit, b in enumerate(levels[n][0]):
            if (d >> at_bit) & 1:
                place = place + (1 - 2 * bit_vals[b]) * (1 << b)
        return (dp, place)

    def digit(n, d):
        value = 0
        for at_bit, b in enumerate(levels[n][0]):
            bit = bit_vals[b]
            value = value + (1 - bit if (d >> at_bit) & 1 else bit) * (1 << at_bit)
        return value

    partners = [core_id, x_id] + [peer_id(n, d) for n, d in exchanges] + [left_id, right_id]
    barrier = pltpu.get_barrier_semaphore()
    for partner in partners:
        pl.semaphore_signal(barrier, inc=1, device_id=partner, device_id_type=MESH)
    pl.semaphore_wait(barrier, len(partners))

    def remote(src, dst, ss, rs, who):
        return pltpu.make_async_remote_copy(
            src_ref=src, dst_ref=dst, send_sem=ss, recv_sem=rs, device_id=who, device_id_type=MESH
        )

    yi = bit_vals[0]
    y_id = bit_ids[0]
    dpx = dp + 2 - 4 * xi
    zi = bit_vals[1]
    z_id = bit_ids[1]
    quarter = depth // 4

    def part_of(p, block, side):
        return wg.at[p, block, pl.ds(pl.multiple_of(side * quarter, 16), quarter)]

    def passed(p, block, side, sem, who):
        part = wg.at[p, block] if side is None else part_of(p, block, side)
        return remote(part, part, w_ss.at[sem * CHUNKS + p], w_rs.at[sem * CHUNKS + p], who)

    here, by_y = 2 * yi + zi, 2 * (1 - yi) + zi
    by_z, by_both = 2 * yi + 1 - zi, 2 * (1 - yi) + 1 - zi
    over_x = lambda p: passed(p, dp, here, 0, x_id)
    own = lambda p: passed(p, dp, None, 1, core_id)
    over_y = lambda p: passed(p, dpx, here, 2, y_id)
    over_z = lambda p: passed(p, dpx, here, 3, z_id)
    over_yz = lambda p: passed(p, dpx, by_y, 4, z_id)
    to_core = [lambda p, n=n, side=side: passed(p, dpx, side, 5 + n, core_id) for n, side in enumerate((here, by_y, by_z, by_both))]
    for p in range(CHUNKS):
        w_loads[p].wait()
        over_x(p).start()
        own(p).start()
    loads[0].wait()
    sends = []
    halo_u = [
        remote(cot_ref.at[pl.ds(rows - EDGE, EDGE)], hu.at[0], h_ss.at[0], h_rs.at[0], right_id),
        remote(cot_ref.at[pl.ds(0, EDGE)], hu.at[1], h_ss.at[1], h_rs.at[1], left_id),
    ]
    for copy in halo_u:
        copy.start()

    tile = LANES
    for copy in loads[1:]:
        copy.wait()
    tok = jnp.broadcast_to(tok_ref[...], (rows, rows)).astype(F32).T
    tok = jnp.concatenate([tok] * (tile // rows), axis=1) if tile > rows else tok[:, :tile]

    def stream_tile(i, carry):
        cols = pl.ds(pl.multiple_of(i * tile, tile), tile)
        looked = jnp.zeros((rows, tile), F32)
        for k in range(vocab):
            looked = looked + jnp.where(tok == float(k), emb_ref[pl.ds(k, 1), cols], 0.0)
        sx[0, pl.ds(EDGE, rows), cols] = (hid_ref[:, cols].astype(F32) + looked).astype(BF16)
        return carry

    lax.fori_loop(0, width // tile, stream_tile, 0)
    halo_s = [
        remote(sx.at[0, pl.ds(rows, EDGE)], hx.at[0], h_ss.at[2], h_rs.at[2], right_id),
        remote(sx.at[0, pl.ds(EDGE, EDGE)], hx.at[1], h_ss.at[3], h_rs.at[3], left_id),
    ]
    for copy in halo_s:
        copy.start()
    sends += halo_u + halo_s

    has_left = (seq > 0).astype(F32)
    has_right = (seq < seq_count - 1).astype(F32)
    ux[0, pl.ds(EDGE, rows), :] = cot_ref[...]
    for copy in halo_u + halo_s:
        copy.wait_recv()
    sx[0, pl.ds(0, EDGE), :] = (hx[0].astype(F32) * has_left).astype(BF16)
    sx[0, pl.ds(rows + EDGE, EDGE), :] = (hx[1].astype(F32) * has_right).astype(BF16)
    ux[0, pl.ds(0, EDGE), :] = (hu[0].astype(F32) * has_left).astype(BF16)
    ux[0, pl.ds(rows + EDGE, EDGE), :] = (hu[1].astype(F32) * has_right).astype(BF16)

    flip = (
        lax.broadcasted_iota(jnp.int32, (tile, tile), 0)
        + lax.broadcasted_iota(jnp.int32, (tile, tile), 1)
        == tile - 1
    ).astype(F32).astype(BF16)

    def mirrored(block):
        return jnp.dot(block, flip, preferred_element_type=F32)

    def reverse_stream(i, carry):
        cols = pl.ds(pl.multiple_of(i * tile, tile), tile)
        back = pl.ds(pl.multiple_of(width - tile - i * tile, tile), tile)
        sx[1, :, back] = mirrored(sx[0, :, cols]).astype(BF16)
        return carry

    lax.fori_loop(0, width // tile, reverse_stream, 0)

    def reverse_up(i, carry):
        cols = pl.ds(pl.multiple_of(i * tile, tile), tile)
        back = pl.ds(pl.multiple_of(units - tile - i * tile, tile), tile)
        ux[1, :, back] = mirrored(ux[0, :, cols]).astype(BF16)
        return carry

    lax.fori_loop(0, units // tile, reverse_up, 0)

    def arrived_x(p):
        over_x(p).wait_recv()
        over_y(p).start()
        over_z(p).start()
        to_core[0](p).start()

    def arrived_y(p):
        over_y(p).wait_recv()
        over_yz(p).start()
        to_core[1](p).start()

    def arrived_z(p):
        over_z(p).wait_recv()
        to_core[2](p).start()
        over_yz(p).wait_recv()
        to_core[3](p).start()

    def transpose_tile(i, carry):
        cols = pl.ds(pl.multiple_of(i * tile, tile), tile)
        for s in range(2):
            s2t[cols, pl.ds(s * rows, rows)] = sx[s, pl.ds(EDGE, rows), cols].T
        return carry

    lax.fori_loop(0, width // tile, transpose_tile, 0)
    stream_copy = remote(
        s2t.at[pl.ds(pl.multiple_of((1 - xi) * 2 * depth, depth), 2 * depth)], s2tp, h_ss.at[4], h_rs.at[4], x_id
    )
    sends.append(stream_copy)

    ew = 128
    lo = EDGE - 8

    rt = 32

    def strand_tile(i, carry):
        cols = pl.ds(pl.multiple_of(i * ew, ew), ew)
        inner = pl.ds(pl.multiple_of((i % (cw // ew)) * ew, ew), ew)
        tap_rows = [ker_ref[pl.ds(k, 1), cols] for k in range(taps)]
        tap_sums = [jnp.zeros((8, ew), F32)] * taps
        for s in range(2):
            for r in range(0, rows + 16, rt // 2):
                at = pl.ds(lo + r, rt // 2)
                part = val[s, at, cols].astype(BF16).astype(F32)
                val[s, at, cols] = part
                logistic = jax.nn.sigmoid(part)
                gate = part * logistic
                sigs[s, pl.ds(r, rt // 2), :] = logistic
                gmix[s, pl.ds(r, rt // 2), :] = ux[s, at, cols].astype(F32) * gate
            for r in range(0, rows, rt):
                lin = val[s, pl.ds(EDGE + r, rt), cols]
                sig = sigs[s, pl.ds(8 + r, rt), :]
                up = ux[s, pl.ds(EDGE + r, rt), cols].astype(F32)
                mine = gmix[s, pl.ds(8 + r, rt), :]
                mixing = jnp.zeros((rt, ew), F32)
                spread = jnp.zeros((rt, ew), F32)
                for m in range(taps):
                    k = m if s == 0 else taps - 1 - m
                    row = tap_rows[k]
                    shifted = val[s, pl.ds(EDGE + r + m - reach, rt), cols]
                    mixing = mixing + row * shifted
                    product_sum = mine * shifted
                    for q in range(0, rt, 8):
                        tap_sums[k] = tap_sums[k] + product_sum[q : q + 8]
                    spread = spread + row * gmix[s, pl.ds(8 + r + reach - m, rt), :]
                strand_out = mixing * (lin * sig)
                if s == 0:
                    outs[pl.ds(r, rt), cols] = strand_out
                else:
                    routs[pl.ds(r, rt), cols] = strand_out.astype(BF16)
                grad = up * mixing * sig * (1.0 + lin * (1.0 - sig)) + spread
                gv[i // (cw // ew), pl.ds(s * rows + r, rt), inner] = grad.astype(BF16)
        tap_sums = [jnp.sum(value, axis=0, keepdims=True) for value in tap_sums]
        small_cols = pl.ds(pl.multiple_of((i % (units // 2 // ew)) * ew, ew), ew)
        pad = [jnp.zeros((1, ew), F32)] * (8 - taps)
        small[i // (units // 2 // ew), pl.ds(0, 8), small_cols] = jnp.concatenate(tap_sums + pad, axis=0)
        return carry

    def elementwise(j):
        @pl.when(j + 2 < CHUNKS)
        def _():
            arrived_x(j + 2)

        @pl.when(j + 3 == CHUNKS)
        def _():
            stream_copy.start()

        @pl.when(j + 1 < CHUNKS)
        def _():
            arrived_y(j + 1)

        arrived_z(j)
        for copy in [own(j)] + [forward(j) for forward in to_core]:
            copy.wait_recv()
        projected = jnp.zeros((2 * total, cw), F32)
        for block in range(wg.shape[1]):
            columns = sx[:, :, pl.ds(block * depth, depth)].reshape(2 * total, depth)
            projected = projected + jnp.dot(columns, wg[j, block], preferred_element_type=F32)
        val[:, :, pl.ds(pl.multiple_of(j * cw, cw), cw)] = projected.reshape(2, total, cw)
        lax.fori_loop(0, cw // ew, lambda q, carry: strand_tile(j * (cw // ew) + q, carry), 0)
        grad_copy(j).start()

    def grad_copy(j):
        return remote(gv.at[j], gvp.at[j], r_ss.at[j, 1], r_rs.at[j, 1], x_id)

    def core_copy(j):
        return remote(core_send.at[j], core_recv.at[j], r_ss.at[j, 0], r_rs.at[j, 0], core_id)

    def product(j):
        @pl.when(j == 0)
        def _():
            stream_copy.wait_recv()

        grad_copy(j).wait_recv()
        for side in range(2):
            block = 1 - ci if side == 0 else ci
            mine = pl.ds(pl.multiple_of((2 * xi + block) * depth, depth), depth)
            theirs = pl.ds(pl.multiple_of(block * depth, depth), depth)
            result = jnp.dot(s2t[mine, :], gv[j], preferred_element_type=F32)
            result = result + jnp.dot(s2tp[theirs, :], gvp[j], preferred_element_type=F32)
            if side == 0:
                core_send[j] = result.astype(BF16)
                core_copy(j).start()
            else:
                acc[j] = result

    def after_core(j):
        core_copy(j).wait_recv()
        acc[j] += core_recv[j].astype(F32)
        rs_start(j, 0)

    bases = [0]
    for n, (_, size, split) in enumerate(levels):
        bases.append(bases[-1] + digit(n, 0) * size if split else bases[-1])

    def rows_at(n, d):
        size, split = levels[n][1:]
        base = bases[n] + digit(n, d) * size if split else bases[n]
        return pl.ds(pl.multiple_of(base, 16), size)

    slots, at = {}, 0
    for n, d in exchanges:
        slots[n, d] = at
        at += levels[n][1]
    number = {pair: k for k, pair in enumerate(exchanges)}
    ways = [[d for m, d in exchanges if m == n] for n in range(len(levels))]

    def rs_copy(j, n, d):
        where = pl.ds(slots[n, d], levels[n][1])
        sem = 2 + number[n, d]
        return remote(seq_send.at[j, where], seq_recv.at[j, where], r_ss.at[j, sem], r_rs.at[j, sem], peer_id(n, d))

    def rs_start(j, n):
        for d in ways[n]:
            seq_send[j, pl.ds(slots[n, d], levels[n][1]), :] = acc[j, rows_at(n, d), :].astype(BF16)
            rs_copy(j, n, d).start()

    def rs_finish(j, n):
        for d in ways[n]:
            rs_copy(j, n, d).wait_recv()
        total_rows = acc[j, rows_at(n, 0), :]
        for d in ways[n]:
            total_rows = total_rows + seq_recv[j, pl.ds(slots[n, d], levels[n][1]), :].astype(F32)
        acc[j, rows_at(n, 0), :] = total_rows

    gathers = [n for n in reversed(range(len(levels))) if levels[n][2]]

    def ag_copy(j, n, d):
        size = levels[n][1]
        ref = gathered.at[j, pl.ds(pl.multiple_of(bases[n + 1], 16), size)]
        sem = 2 + len(exchanges) + number[n, d]
        return remote(ref, ref, r_ss.at[j, sem], r_rs.at[j, sem], peer_id(n, d))

    def ag_start(j, n):
        for d in ways[n]:
            ag_copy(j, n, d).start()

    def stages(j):
        def after_rs(n):
            rs_finish(j, n)
            if n + 1 < len(levels):
                rs_start(j, n + 1)
            else:
                last = rows_at(n, 0)
                gathered[j, last, :] = acc[j, last, :].astype(BF16)
                ag_start(j, gathers[0])

        def after_ag(k):
            for d in ways[gathers[k]]:
                ag_copy(j, gathers[k], d).wait_recv()
            if k + 1 < len(gathers):
                ag_start(j, gathers[k + 1])
            else:
                gw_ref[:, pl.ds(pl.multiple_of(j * cw, cw), cw)] = gathered[j]

        steps = [functools.partial(stage, j) for stage in (product, after_core)]
        steps += [functools.partial(after_rs, b) for b in range(len(levels))]
        steps += [functools.partial(after_ag, n) for n in range(len(gathers))]
        return steps

    def back_tile(i, carry):
        b = i // (depth // tile)
        r = pl.ds(pl.multiple_of((i % (depth // tile)) * tile, tile), tile)
        cols = pl.ds(pl.multiple_of(i * tile, tile), tile)
        mirror = pl.ds(pl.multiple_of(width - tile - i * tile, tile), tile)
        part = jnp.zeros((2 * rows, tile), F32)
        for j in range(CHUNKS):
            part = part + lax.dot_general(
                gv[j], wg[j, b, r, :], (((1,), (1,)), ((), ())), preferred_element_type=F32
            )
        fwd_back[:, cols] = part[:rows]
        rev_back[:, mirror] = mirrored(part[rows:].astype(BF16))
        return carry

    one_hot = (
        lax.broadcasted_iota(jnp.int32, (8, rows), 0) == tok_ref[...]
    ).astype(F32).astype(BF16)

    def input_tile(i, carry):
        cols = pl.ds(pl.multiple_of(i * tile, tile), tile)
        grad = fwd_back[:, cols] + rev_back[:, cols]
        top = grad.astype(BF16)
        hout_ref[:, cols] = top
        left = grad - top.astype(F32)
        mid = left.astype(BF16)
        low = (left - mid.astype(F32)).astype(BF16)
        table = jnp.dot(one_hot, top, preferred_element_type=F32)
        table = table + jnp.dot(one_hot, mid, preferred_element_type=F32)
        table = table + jnp.dot(one_hot, low, preferred_element_type=F32)
        per = units // 2 // tile
        where = pl.ds(pl.multiple_of((i % per) * tile, tile), tile)
        at_rows = pl.ds(pl.multiple_of(8 + 8 * ((i // per) % 2), 8), 8)
        small[i // (2 * per), at_rows, where] = table
        return carry


    small_ids = [core_id, x_id] + bit_ids

    def small_copy(n):
        src = small.at[1 - ci] if n == 0 else small.at[2 + (n - 1) % 2]
        return remote(src, small_recv.at[n], s_ss.at[n], s_rs.at[n], small_ids[n])

    def small_last():
        return remote(small_ref.at[ci], small_ref.at[ci], s_ss.at[bits + 2], s_rs.at[bits + 2], core_id)

    def small_step(n):
        small_copy(n).wait_recv()
        base = small[ci] if n == 0 else small[2 + (n - 1) % 2]
        now = base + small_recv[n]
        if n < bits + 1:
            if n >= 2:
                small_copy(n - 1).wait_send()
            small[2 + n % 2] = now
            small_copy(n + 1).start()
        else:
            small_ref[ci] = now
            small_last().start()

    def result_tile(i, carry):
        cols = pl.ds(pl.multiple_of(i * tile, tile), tile)
        mirror = pl.ds(pl.multiple_of(units - tile - i * tile, tile), tile)
        block_ref[:, cols] = (outs[:, cols] + mirrored(routs[:, mirror])).astype(BF16)
        return carry

    tiles = width // tile

    def fill_input():
        lax.fori_loop(0, tiles, input_tile, 0)
        small_copy(0).start()

    def fill_result():
        lax.fori_loop(0, units // tile, result_tile, 0)
        small_step(0)

    arrived_x(0)
    arrived_x(1)
    arrived_y(0)

    def elementwise_step(j, carry):
        elementwise(j)
        return carry

    lax.fori_loop(0, CHUNKS, elementwise_step, 0)
    lax.fori_loop(0, tiles, back_tile, 0)

    fillers = [fill_input, fill_result] + [functools.partial(small_step, n) for n in range(1, bits + 2)]
    length = len(stages(0))
    waves = length + CHUNKS - 1

    def wave_step(wave, carry):
        for at_stage in reversed(range(length)):
            j = wave - at_stage

            @pl.when((j >= 0) & (j < CHUNKS))
            def _():
                stages(j)[at_stage]()

        for n, filler in enumerate(fillers[:waves]):
            pl.when(wave == n)(filler)
        return carry

    lax.fori_loop(0, waves, wave_step, 0)
    for filler in fillers[waves:]:
        filler()
    small_last().wait_recv()
    for h in range(2):
        kernel_ref[:, pl.ds(h * units // 2, units // 2)] = small_ref[h, :taps, :] * factor
        for q in range(2):
            columns = pl.ds((2 * h + q) * (units // 2), units // 2)
            table_ref[:, columns] = small_ref[h, 8 + 8 * q : 8 + 8 * q + vocab, :] * factor

    for copy in sends:
        copy.wait_send()

    def drain(j, carry):
        for copy in [over_x(j), own(j), over_y(j), over_z(j), over_yz(j), core_copy(j), grad_copy(j)]:
            copy.wait_send()
        for forward in to_core:
            forward(j).wait_send()
        for n, d in exchanges:
            rs_copy(j, n, d).wait_send()
            if levels[n][2]:
                ag_copy(j, n, d).wait_send()
        return carry

    lax.fori_loop(0, CHUNKS, drain, 0)
    small_copy(0).wait_send()
    small_copy(bits).wait_send()
    small_copy(bits + 1).wait_send()
    small_last().wait_send()


def finish(factor, b_in, h_in, g_in, k_in, t_in, b_out, h_out, g_out, k_out, t_out, b_mid, h_mid, k_mid, t_mid, narrow, wide, sems):
    step = g_in.shape[0] // 4
    parts = [pl.ds(q * step, step) for q in range(4)]
    inward = [(g_in.at[part], narrow.at[part]) for part in parts]
    inward += [(h_in, h_mid), (b_in, b_mid), (t_in, t_mid), (k_in, k_mid)]
    outward = [(wide.at[part], g_out.at[part]) for part in parts]
    outward += [(h_mid, h_out), (b_mid, b_out), (t_mid, t_out), (k_mid, k_out)]
    fetches = [pltpu.make_async_copy(src, dst, sems.at[n]) for n, (src, dst) in enumerate(inward)]
    stores = [pltpu.make_async_copy(src, dst, sems.at[8 + n]) for n, (src, dst) in enumerate(outward)]
    for copy in fetches:
        copy.start()
    for n in range(8):
        fetches[n].wait()
        if n < 4:
            wide[parts[n], :] = narrow[parts[n], :].astype(F32) * factor
        stores[n].start()
    for copy in stores:
        copy.wait()


def local(seq_count, hidden, tokens, embedding, weight, kernel, cotangent):
    window, token_codes, upstream = hidden[0], tokens[0], cotangent[0]
    rows, width = window.shape
    depth, units = weight.shape
    blocks = width // depth
    taps, vocab = kernel.shape[0], embedding.shape[0]
    bits = seq_count.bit_length() - 1
    positions = hidden.shape[0] * rows * lax.axis_size("dp") * seq_count
    total = rows + 2 * EDGE
    cw = units // CHUNKS
    factor = 1.0 / math.sqrt(positions)
    levels = level_plan(depth, bits)
    stacked_rows = sum(size * ((1 << len(group)) - 1) for group, size, _ in levels)
    copies = sum((1 << len(group)) - 1 for group, _, _ in levels)
    vmem = pl.BlockSpec(memory_space=pltpu.VMEM)
    dma = pltpu.SemaphoreType.DMA
    block_result, grad_hidden, grad_weight, kernel_sum, table = pl.pallas_call(
        functools.partial(body, seq_count, bits, factor),
        out_shape=(
            jax.ShapeDtypeStruct((rows, units), BF16),
            jax.ShapeDtypeStruct((rows, width), BF16),
            jax.ShapeDtypeStruct((depth, units), BF16),
            jax.ShapeDtypeStruct((taps, units), F32),
            jax.ShapeDtypeStruct((vocab, width), F32),
        ),
        in_specs=[pl.BlockSpec(memory_space=pltpu.HBM)] * 6,
        out_specs=(vmem,) * 5,
        scratch_shapes=[
            pltpu.VMEM((rows, width), BF16),
            pltpu.VMEM((1, rows), jnp.int32),
            pltpu.VMEM((vocab, width), F32),
            pltpu.VMEM((taps, units), F32),
            pltpu.VMEM((rows, units), BF16),
            pltpu.VMEM((CHUNKS, blocks, depth, cw), BF16),
            pltpu.VMEM((2, total, width), BF16),
            pltpu.VMEM((2, EDGE, width), BF16),
            pltpu.VMEM((2, total, units), BF16),
            pltpu.VMEM((2, EDGE, units), BF16),
            pltpu.VMEM((width, 2 * rows), BF16),
            pltpu.VMEM((2 * depth, 2 * rows), BF16),
            pltpu.VMEM((2, total, units), F32),
            pltpu.VMEM((2, rows + 16, 128), F32),
            pltpu.VMEM((2, rows + 16, 128), F32),
            pltpu.VMEM((rows, units), F32),
            pltpu.VMEM((rows, units), BF16),
            pltpu.VMEM((CHUNKS, 2 * rows, cw), BF16),
            pltpu.VMEM((CHUNKS, 2 * rows, cw), BF16),
            pltpu.VMEM((rows, width), F32),
            pltpu.VMEM((rows, width), F32),
            pltpu.VMEM((CHUNKS, depth, cw), F32),
            pltpu.VMEM((CHUNKS, depth, cw), BF16),
            pltpu.VMEM((CHUNKS, depth, cw), BF16),
            pltpu.VMEM((CHUNKS, stacked_rows, cw), BF16),
            pltpu.VMEM((CHUNKS, stacked_rows, cw), BF16),
            pltpu.VMEM((CHUNKS, depth, cw), BF16),
            pltpu.VMEM((4, 24, units // 2), F32),
            pltpu.VMEM((bits + 2, 24, units // 2), F32),
            pltpu.VMEM((2, 24, units // 2), F32),
            dma((5 + CHUNKS,)),
            dma((9 * CHUNKS,)), dma((9 * CHUNKS,)),
            dma((5,)), dma((5,)),
            dma((CHUNKS, 2 + 2 * copies)), dma((CHUNKS, 2 + 2 * copies)),
            dma((bits + 3,)), dma((bits + 3,)),
        ],
        compiler_params=pltpu.CompilerParams(
            collective_id=0, has_side_effects=True, vmem_limit_bytes=60 * 1024 * 1024
        ),
        cost_estimate=pl.CostEstimate(
            flops=12 * rows * width * units, bytes_accessed=8 * rows * width, transcendentals=4 * rows * units
        ),
    )(
        window,
        token_codes.reshape(1, rows),
        embedding,
        weight,
        kernel,
        upstream,
    )
    block_result, grad_hidden, grad_weight, kernel_sum, table = pl.pallas_call(
        functools.partial(finish, factor),
        out_shape=(
            jax.ShapeDtypeStruct((rows, units), BF16),
            jax.ShapeDtypeStruct((rows, width), BF16),
            jax.ShapeDtypeStruct((depth, units), F32),
            jax.ShapeDtypeStruct((taps, units), F32),
            jax.ShapeDtypeStruct((vocab, width), F32),
        ),
        in_specs=[pl.BlockSpec(memory_space=pltpu.HBM)] * 5,
        out_specs=(pl.BlockSpec(memory_space=pltpu.HBM),) * 5,
        scratch_shapes=[
            pltpu.VMEM((rows, units), BF16),
            pltpu.VMEM((rows, width), BF16),
            pltpu.VMEM((taps, units), F32),
            pltpu.VMEM((vocab, width), F32),
            pltpu.VMEM((depth, units), BF16),
            pltpu.VMEM((depth, units), F32),
            dma((16,)),
        ],
        compiler_params=pltpu.CompilerParams(vmem_limit_bytes=60 * 1024 * 1024),
    )(block_result, grad_hidden, grad_weight, kernel_sum, table)
    return (
        block_result[None],
        grad_hidden[None],
        grad_weight,
        kernel_sum,
        table,
    )


def solution(mesh):
    in_specs = (P("dp", "seq", None), P("dp", "seq"), P(), P("dp", None), P(), P("dp", "seq", None))
    out_specs = (P("dp", "seq", None), P("dp", "seq", None), P("dp", None), P(), P())
    return jax.shard_map(
        functools.partial(local, mesh.shape["seq"]),
        mesh=mesh, in_specs=in_specs, out_specs=out_specs, check_vma=False,
    )
```

```python
import functools
import math

import jax
import jax.numpy as jnp
from jax import lax
from jax.experimental import pallas as pl
from jax.experimental.pallas import tpu as pltpu
from jax.sharding import PartitionSpec as P

MESH = pl.DeviceIdType.MESH
F32 = jnp.float32
BF16 = jnp.bfloat16
EDGE = 16
CHUNKS = 2
LANES = 256


def level_plan(rows, bits):
    groups = [[0], [1, 2]] + [[b] for b in range(3, bits)] if bits >= 3 else [[b] for b in range(bits)]
    levels = []
    for group in groups:
        ways = 1 << len(group)
        split = rows % (16 * ways) == 0
        if split:
            rows //= ways
            levels.append((group, rows, True))
        else:
            levels += [([b], rows, False) for b in group]
    return levels


def body(
    seq_count, bits, factor,
    hid_in, tok_in, emb_in, w_in, ker_in, cot_in,
    block_ref, hout_ref, gw_ref, kernel_ref, table_ref,
    hid_ref, tok_ref, emb_ref, ker_ref, cot_ref,
    wg, sx, hx, ux, hu, s2t, s2tp, val, gmix, sigs, outs, routs, gv, gvp, fwd_back, rev_back,
    acc, core_send, core_recv, seq_send, seq_recv, gathered,
    small, small_recv, small_ref,
    in_sems, w_ss, w_rs, h_ss, h_rs, r_ss, r_rs, s_ss, s_rs,
):
    rows = hid_ref.shape[0]
    depth, units = w_in.shape
    width = hid_ref.shape[1]
    taps = ker_ref.shape[0]
    reach = (taps - 1) // 2
    vocab = emb_ref.shape[0]
    total = rows + 2 * EDGE
    dp = lax.axis_index("dp")
    seq = lax.axis_index("seq")
    xi, ci = dp // 2, dp % 2
    cw = units // CHUNKS
    w_loads = [
        pltpu.make_async_copy(w_in.at[:, pl.ds(p * cw, cw)], wg.at[p, dp], in_sems.at[5 + p]) for p in range(CHUNKS)
    ]
    loads = [
        pltpu.make_async_copy(src, dst, in_sems.at[n])
        for n, (src, dst) in enumerate(
            [(cot_in, cot_ref), (hid_in, hid_ref), (tok_in, tok_ref), (emb_in, emb_ref), (ker_in, ker_ref)]
        )
    ]
    for copy in w_loads + loads:
        copy.start()
    core_id = (dp + 1 - 2 * ci, seq)
    x_id = (dp + 2 - 4 * xi, seq)
    bit_vals = [(seq // (1 << b)) % 2 for b in range(bits)]
    bit_ids = [(dp, seq + (1 - 2 * bit_vals[b]) * (1 << b)) for b in range(bits)]
    left_id = (dp, (seq + seq_count - 1) % seq_count)
    right_id = (dp, (seq + 1) % seq_count)

    levels = level_plan(depth, bits)
    exchanges = [(n, d) for n, (group, _, _) in enumerate(levels) for d in range(1, 1 << len(group))]

    def peer_id(n, d):
        place = seq
        for at_bit, b in enumerate(levels[n][0]):
            if (d >> at_bit) & 1:
                place = place + (1 - 2 * bit_vals[b]) * (1 << b)
        return (dp, place)

    def digit(n, d):
        value = 0
        for at_bit, b in enumerate(levels[n][0]):
            bit = bit_vals[b]
            value = value + (1 - bit if (d >> at_bit) & 1 else bit) * (1 << at_bit)
        return value

    partners = [core_id, x_id] + [peer_id(n, d) for n, d in exchanges] + [left_id, right_id]
    barrier = pltpu.get_barrier_semaphore()
    for partner in partners:
        pl.semaphore_signal(barrier, inc=1, device_id=partner, device_id_type=MESH)
    pl.semaphore_wait(barrier, len(partners))

    def remote(src, dst, ss, rs, who):
        return pltpu.make_async_remote_copy(
            src_ref=src, dst_ref=dst, send_sem=ss, recv_sem=rs, device_id=who, device_id_type=MESH
        )

    yi = bit_vals[0]
    y_id = bit_ids[0]
    dpx = dp + 2 - 4 * xi
    half = depth // 2

    def part_of(p, block, side):
        return wg.at[p, block, pl.ds(pl.multiple_of(side * half, 16), half)]

    def passed(p, block, side, sem, who):
        part = wg.at[p, block] if side is None else part_of(p, block, side)
        return remote(part, part, w_ss.at[sem * CHUNKS + p], w_rs.at[sem * CHUNKS + p], who)

    over_x = lambda p: passed(p, dp, yi, 0, x_id)
    own = lambda p: passed(p, dp, None, 1, core_id)
    over_y = lambda p: passed(p, dpx, yi, 2, y_id)
    over_core = lambda p: passed(p, dpx, yi, 3, core_id)
    over_core2 = lambda p: passed(p, dpx, 1 - yi, 4, core_id)
    for p in range(CHUNKS):
        w_loads[p].wait()
        over_x(p).start()
        own(p).start()
    loads[0].wait()
    sends = []
    halo_u = [
        remote(cot_ref.at[pl.ds(rows - EDGE, EDGE)], hu.at[0], h_ss.at[0], h_rs.at[0], right_id),
        remote(cot_ref.at[pl.ds(0, EDGE)], hu.at[1], h_ss.at[1], h_rs.at[1], left_id),
    ]
    for copy in halo_u:
        copy.start()

    tile = LANES
    for copy in loads[1:]:
        copy.wait()
    tok = jnp.broadcast_to(tok_ref[...], (rows, rows)).astype(F32).T
    tok = jnp.concatenate([tok] * (tile // rows), axis=1) if tile > rows else tok[:, :tile]

    def stream_tile(i, carry):
        cols = pl.ds(pl.multiple_of(i * tile, tile), tile)
        looked = jnp.zeros((rows, tile), F32)
        for k in range(vocab):
            looked = looked + jnp.where(tok == float(k), emb_ref[pl.ds(k, 1), cols], 0.0)
        sx[0, pl.ds(EDGE, rows), cols] = (hid_ref[:, cols].astype(F32) + looked).astype(BF16)
        return carry

    lax.fori_loop(0, width // tile, stream_tile, 0)
    halo_s = [
        remote(sx.at[0, pl.ds(rows, EDGE)], hx.at[0], h_ss.at[2], h_rs.at[2], right_id),
        remote(sx.at[0, pl.ds(EDGE, EDGE)], hx.at[1], h_ss.at[3], h_rs.at[3], left_id),
    ]
    for copy in halo_s:
        copy.start()
    sends += halo_u + halo_s

    has_left = (seq > 0).astype(F32)
    has_right = (seq < seq_count - 1).astype(F32)
    ux[0, pl.ds(EDGE, rows), :] = cot_ref[...]
    for copy in halo_u + halo_s:
        copy.wait_recv()
    sx[0, pl.ds(0, EDGE), :] = (hx[0].astype(F32) * has_left).astype(BF16)
    sx[0, pl.ds(rows + EDGE, EDGE), :] = (hx[1].astype(F32) * has_right).astype(BF16)
    ux[0, pl.ds(0, EDGE), :] = (hu[0].astype(F32) * has_left).astype(BF16)
    ux[0, pl.ds(rows + EDGE, EDGE), :] = (hu[1].astype(F32) * has_right).astype(BF16)

    flip = (
        lax.broadcasted_iota(jnp.int32, (tile, tile), 0)
        + lax.broadcasted_iota(jnp.int32, (tile, tile), 1)
        == tile - 1
    ).astype(F32).astype(BF16)

    def mirrored(block):
        return jnp.dot(block, flip, preferred_element_type=F32)

    def reverse_stream(i, carry):
        cols = pl.ds(pl.multiple_of(i * tile, tile), tile)
        back = pl.ds(pl.multiple_of(width - tile - i * tile, tile), tile)
        sx[1, :, back] = mirrored(sx[0, :, cols]).astype(BF16)
        return carry

    lax.fori_loop(0, width // tile, reverse_stream, 0)

    def reverse_up(i, carry):
        cols = pl.ds(pl.multiple_of(i * tile, tile), tile)
        back = pl.ds(pl.multiple_of(units - tile - i * tile, tile), tile)
        ux[1, :, back] = mirrored(ux[0, :, cols]).astype(BF16)
        return carry

    lax.fori_loop(0, units // tile, reverse_up, 0)

    def arrived_x(p):
        over_x(p).wait_recv()
        over_y(p).start()
        over_core(p).start()

    def arrived_y(p):
        over_y(p).wait_recv()
        over_core2(p).start()

    def transpose_tile(i, carry):
        cols = pl.ds(pl.multiple_of(i * tile, tile), tile)
        for s in range(2):
            s2t[cols, pl.ds(s * rows, rows)] = sx[s, pl.ds(EDGE, rows), cols].T
        return carry

    lax.fori_loop(0, width // tile, transpose_tile, 0)
    stream_copy = remote(
        s2t.at[pl.ds(pl.multiple_of((1 - xi) * 2 * depth, depth), 2 * depth)], s2tp, h_ss.at[4], h_rs.at[4], x_id
    )
    sends.append(stream_copy)

    ew = 128
    lo = EDGE - 8

    rt = 32

    def strand_tile(i, carry):
        cols = pl.ds(pl.multiple_of(i * ew, ew), ew)
        inner = pl.ds(pl.multiple_of((i % (cw // ew)) * ew, ew), ew)
        tap_rows = [ker_ref[pl.ds(k, 1), cols] for k in range(taps)]
        tap_sums = [jnp.zeros((8, ew), F32)] * taps
        for s in range(2):
            for r in range(0, rows + 16, rt // 2):
                at = pl.ds(lo + r, rt // 2)
                part = val[s, at, cols].astype(BF16).astype(F32)
                val[s, at, cols] = part
                logistic = jax.nn.sigmoid(part)
                gate = part * logistic
                sigs[s, pl.ds(r, rt // 2), :] = logistic
                gmix[s, pl.ds(r, rt // 2), :] = ux[s, at, cols].astype(F32) * gate
            for r in range(0, rows, rt):
                lin = val[s, pl.ds(EDGE + r, rt), cols]
                sig = sigs[s, pl.ds(8 + r, rt), :]
                up = ux[s, pl.ds(EDGE + r, rt), cols].astype(F32)
                mine = gmix[s, pl.ds(8 + r, rt), :]
                mixing = jnp.zeros((rt, ew), F32)
                spread = jnp.zeros((rt, ew), F32)
                for m in range(taps):
                    k = m if s == 0 else taps - 1 - m
                    row = tap_rows[k]
                    shifted = val[s, pl.ds(EDGE + r + m - reach, rt), cols]
                    mixing = mixing + row * shifted
                    product_sum = mine * shifted
                    for q in range(0, rt, 8):
                        tap_sums[k] = tap_sums[k] + product_sum[q : q + 8]
                    spread = spread + row * gmix[s, pl.ds(8 + r + reach - m, rt), :]
                strand_out = mixing * (lin * sig)
                if s == 0:
                    outs[pl.ds(r, rt), cols] = strand_out
                else:
                    routs[pl.ds(r, rt), cols] = strand_out.astype(BF16)
                grad = up * mixing * sig * (1.0 + lin * (1.0 - sig)) + spread
                gv[i // (cw // ew), pl.ds(s * rows + r, rt), inner] = grad.astype(BF16)
        tap_sums = [jnp.sum(value, axis=0, keepdims=True) for value in tap_sums]
        small_cols = pl.ds(pl.multiple_of((i % (units // 2 // ew)) * ew, ew), ew)
        pad = [jnp.zeros((1, ew), F32)] * (8 - taps)
        small[i // (units // 2 // ew), pl.ds(0, 8), small_cols] = jnp.concatenate(tap_sums + pad, axis=0)
        return carry

    def elementwise(j):
        @pl.when(j + 1 < CHUNKS)
        def _():
            arrived_x(j + 1)

        @pl.when(j + 2 == CHUNKS)
        def _():
            stream_copy.start()

        arrived_y(j)
        for copy in (own(j), over_core(j), over_core2(j)):
            copy.wait_recv()
        projected = jnp.zeros((2 * total, cw), F32)
        for block in range(wg.shape[1]):
            columns = sx[:, :, pl.ds(block * depth, depth)].reshape(2 * total, depth)
            projected = projected + jnp.dot(columns, wg[j, block], preferred_element_type=F32)
        val[:, :, pl.ds(pl.multiple_of(j * cw, cw), cw)] = projected.reshape(2, total, cw)
        lax.fori_loop(0, cw // ew, lambda q, carry: strand_tile(j * (cw // ew) + q, carry), 0)
        grad_copy(j).start()

    def grad_copy(j):
        return remote(gv.at[j], gvp.at[j], r_ss.at[j, 1], r_rs.at[j, 1], x_id)

    def core_copy(j):
        return remote(core_send.at[j], core_recv.at[j], r_ss.at[j, 0], r_rs.at[j, 0], core_id)

    def product(j):
        @pl.when(j == 0)
        def _():
            stream_copy.wait_recv()

        grad_copy(j).wait_recv()
        for side in range(2):
            block = 1 - ci if side == 0 else ci
            mine = pl.ds(pl.multiple_of((2 * xi + block) * depth, depth), depth)
            theirs = pl.ds(pl.multiple_of(block * depth, depth), depth)
            result = jnp.dot(s2t[mine, :], gv[j], preferred_element_type=F32)
            result = result + jnp.dot(s2tp[theirs, :], gvp[j], preferred_element_type=F32)
            if side == 0:
                core_send[j] = result.astype(BF16)
                core_copy(j).start()
            else:
                acc[j] = result

    def after_core(j):
        core_copy(j).wait_recv()
        acc[j] += core_recv[j].astype(F32)
        rs_start(j, 0)

    bases = [0]
    for n, (_, size, split) in enumerate(levels):
        bases.append(bases[-1] + digit(n, 0) * size if split else bases[-1])

    def rows_at(n, d):
        size, split = levels[n][1:]
        base = bases[n] + digit(n, d) * size if split else bases[n]
        return pl.ds(pl.multiple_of(base, 16), size)

    slots, at = {}, 0
    for n, d in exchanges:
        slots[n, d] = at
        at += levels[n][1]
    number = {pair: k for k, pair in enumerate(exchanges)}
    ways = [[d for m, d in exchanges if m == n] for n in range(len(levels))]

    def rs_copy(j, n, d):
        where = pl.ds(slots[n, d], levels[n][1])
        sem = 2 + number[n, d]
        return remote(seq_send.at[j, where], seq_recv.at[j, where], r_ss.at[j, sem], r_rs.at[j, sem], peer_id(n, d))

    def rs_start(j, n):
        for d in ways[n]:
            seq_send[j, pl.ds(slots[n, d], levels[n][1]), :] = acc[j, rows_at(n, d), :].astype(BF16)
            rs_copy(j, n, d).start()

    def rs_finish(j, n):
        for d in ways[n]:
            rs_copy(j, n, d).wait_recv()
        total_rows = acc[j, rows_at(n, 0), :]
        for d in ways[n]:
            total_rows = total_rows + seq_recv[j, pl.ds(slots[n, d], levels[n][1]), :].astype(F32)
        acc[j, rows_at(n, 0), :] = total_rows

    gathers = [n for n in reversed(range(len(levels))) if levels[n][2]]

    def ag_copy(j, n, d):
        size = levels[n][1]
        ref = gathered.at[j, pl.ds(pl.multiple_of(bases[n + 1], 16), size)]
        sem = 2 + len(exchanges) + number[n, d]
        return remote(ref, ref, r_ss.at[j, sem], r_rs.at[j, sem], peer_id(n, d))

    def ag_start(j, n):
        for d in ways[n]:
            ag_copy(j, n, d).start()

    def stages(j):
        def after_rs(n):
            rs_finish(j, n)
            if n + 1 < len(levels):
                rs_start(j, n + 1)
            else:
                last = rows_at(n, 0)
                gathered[j, last, :] = acc[j, last, :].astype(BF16)
                ag_start(j, gathers[0])

        def after_ag(k):
            for d in ways[gathers[k]]:
                ag_copy(j, gathers[k], d).wait_recv()
            if k + 1 < len(gathers):
                ag_start(j, gathers[k + 1])
            else:
                gw_ref[:, pl.ds(pl.multiple_of(j * cw, cw), cw)] = gathered[j]

        steps = [functools.partial(stage, j) for stage in (product, after_core)]
        steps += [functools.partial(after_rs, b) for b in range(len(levels))]
        steps += [functools.partial(after_ag, n) for n in range(len(gathers))]
        return steps

    def back_tile(i, carry):
        b = i // (depth // tile)
        r = pl.ds(pl.multiple_of((i % (depth // tile)) * tile, tile), tile)
        cols = pl.ds(pl.multiple_of(i * tile, tile), tile)
        mirror = pl.ds(pl.multiple_of(width - tile - i * tile, tile), tile)
        part = jnp.zeros((2 * rows, tile), F32)
        for j in range(CHUNKS):
            part = part + lax.dot_general(
                gv[j], wg[j, b, r, :], (((1,), (1,)), ((), ())), preferred_element_type=F32
            )
        fwd_back[:, cols] = part[:rows]
        rev_back[:, mirror] = mirrored(part[rows:].astype(BF16))
        return carry

    one_hot = (
        lax.broadcasted_iota(jnp.int32, (8, rows), 0) == tok_ref[...]
    ).astype(F32).astype(BF16)

    def input_tile(i, carry):
        cols = pl.ds(pl.multiple_of(i * tile, tile), tile)
        grad = fwd_back[:, cols] + rev_back[:, cols]
        top = grad.astype(BF16)
        hout_ref[:, cols] = top
        left = grad - top.astype(F32)
        mid = left.astype(BF16)
        low = (left - mid.astype(F32)).astype(BF16)
        table = jnp.dot(one_hot, top, preferred_element_type=F32)
        table = table + jnp.dot(one_hot, mid, preferred_element_type=F32)
        table = table + jnp.dot(one_hot, low, preferred_element_type=F32)
        per = units // 2 // tile
        where = pl.ds(pl.multiple_of((i % per) * tile, tile), tile)
        at_rows = pl.ds(pl.multiple_of(8 + 8 * ((i // per) % 2), 8), 8)
        small[i // (2 * per), at_rows, where] = table
        return carry


    small_ids = [core_id, x_id] + bit_ids

    def small_copy(n):
        src = small.at[1 - ci] if n == 0 else small.at[2 + (n - 1) % 2]
        return remote(src, small_recv.at[n], s_ss.at[n], s_rs.at[n], small_ids[n])

    def small_last():
        return remote(small_ref.at[ci], small_ref.at[ci], s_ss.at[bits + 2], s_rs.at[bits + 2], core_id)

    def small_step(n):
        small_copy(n).wait_recv()
        base = small[ci] if n == 0 else small[2 + (n - 1) % 2]
        now = base + small_recv[n]
        if n < bits + 1:
            if n >= 2:
                small_copy(n - 1).wait_send()
            small[2 + n % 2] = now
            small_copy(n + 1).start()
        else:
            small_ref[ci] = now
            small_last().start()

    def result_tile(i, carry):
        cols = pl.ds(pl.multiple_of(i * tile, tile), tile)
        mirror = pl.ds(pl.multiple_of(units - tile - i * tile, tile), tile)
        block_ref[:, cols] = (outs[:, cols] + mirrored(routs[:, mirror])).astype(BF16)
        return carry

    tiles = width // tile

    def fill_input():
        lax.fori_loop(0, tiles, input_tile, 0)
        small_copy(0).start()

    def fill_result():
        lax.fori_loop(0, units // tile, result_tile, 0)
        small_step(0)

    arrived_x(0)

    def elementwise_step(j, carry):
        elementwise(j)
        return carry

    lax.fori_loop(0, CHUNKS, elementwise_step, 0)
    lax.fori_loop(0, tiles, back_tile, 0)

    fillers = [fill_input, fill_result] + [functools.partial(small_step, n) for n in range(1, bits + 2)]
    length = len(stages(0))
    waves = length + CHUNKS - 1

    def wave_step(wave, carry):
        for at_stage in reversed(range(length)):
            j = wave - at_stage

            @pl.when((j >= 0) & (j < CHUNKS))
            def _():
                stages(j)[at_stage]()

        for n, filler in enumerate(fillers[:waves]):
            pl.when(wave == n)(filler)
        return carry

    lax.fori_loop(0, waves, wave_step, 0)
    for filler in fillers[waves:]:
        filler()
    small_last().wait_recv()
    for h in range(2):
        kernel_ref[:, pl.ds(h * units // 2, units // 2)] = small_ref[h, :taps, :] * factor
        for q in range(2):
            columns = pl.ds((2 * h + q) * (units // 2), units // 2)
            table_ref[:, columns] = small_ref[h, 8 + 8 * q : 8 + 8 * q + vocab, :] * factor

    for copy in sends:
        copy.wait_send()

    def drain(j, carry):
        for copy in (over_x(j), own(j), over_y(j), over_core(j), over_core2(j), core_copy(j), grad_copy(j)):
            copy.wait_send()
        for n, d in exchanges:
            rs_copy(j, n, d).wait_send()
            if levels[n][2]:
                ag_copy(j, n, d).wait_send()
        return carry

    lax.fori_loop(0, CHUNKS, drain, 0)
    small_copy(0).wait_send()
    small_copy(bits).wait_send()
    small_copy(bits + 1).wait_send()
    small_last().wait_send()


def finish(factor, b_in, h_in, g_in, k_in, t_in, b_out, h_out, g_out, k_out, t_out, b_mid, h_mid, k_mid, t_mid, narrow, wide, sems):
    step = g_in.shape[0] // 4
    parts = [pl.ds(q * step, step) for q in range(4)]
    inward = [(g_in.at[part], narrow.at[part]) for part in parts]
    inward += [(h_in, h_mid), (b_in, b_mid), (t_in, t_mid), (k_in, k_mid)]
    outward = [(wide.at[part], g_out.at[part]) for part in parts]
    outward += [(h_mid, h_out), (b_mid, b_out), (t_mid, t_out), (k_mid, k_out)]
    fetches = [pltpu.make_async_copy(src, dst, sems.at[n]) for n, (src, dst) in enumerate(inward)]
    stores = [pltpu.make_async_copy(src, dst, sems.at[8 + n]) for n, (src, dst) in enumerate(outward)]
    for copy in fetches:
        copy.start()
    for n in range(8):
        fetches[n].wait()
        if n < 4:
            wide[parts[n], :] = narrow[parts[n], :].astype(F32) * factor
        stores[n].start()
    for copy in stores:
        copy.wait()


def local(seq_count, hidden, tokens, embedding, weight, kernel, cotangent):
    window, token_codes, upstream = hidden[0], tokens[0], cotangent[0]
    rows, width = window.shape
    depth, units = weight.shape
    blocks = width // depth
    taps, vocab = kernel.shape[0], embedding.shape[0]
    bits = seq_count.bit_length() - 1
    positions = hidden.shape[0] * rows * lax.axis_size("dp") * seq_count
    total = rows + 2 * EDGE
    cw = units // CHUNKS
    factor = 1.0 / math.sqrt(positions)
    levels = level_plan(depth, bits)
    stacked_rows = sum(size * ((1 << len(group)) - 1) for group, size, _ in levels)
    copies = sum((1 << len(group)) - 1 for group, _, _ in levels)
    vmem = pl.BlockSpec(memory_space=pltpu.VMEM)
    dma = pltpu.SemaphoreType.DMA
    block_result, grad_hidden, grad_weight, kernel_sum, table = pl.pallas_call(
        functools.partial(body, seq_count, bits, factor),
        out_shape=(
            jax.ShapeDtypeStruct((rows, units), BF16),
            jax.ShapeDtypeStruct((rows, width), BF16),
            jax.ShapeDtypeStruct((depth, units), BF16),
            jax.ShapeDtypeStruct((taps, units), F32),
            jax.ShapeDtypeStruct((vocab, width), F32),
        ),
        in_specs=[pl.BlockSpec(memory_space=pltpu.HBM)] * 6,
        out_specs=(vmem,) * 5,
        scratch_shapes=[
            pltpu.VMEM((rows, width), BF16),
            pltpu.VMEM((1, rows), jnp.int32),
            pltpu.VMEM((vocab, width), F32),
            pltpu.VMEM((taps, units), F32),
            pltpu.VMEM((rows, units), BF16),
            pltpu.VMEM((CHUNKS, blocks, depth, cw), BF16),
            pltpu.VMEM((2, total, width), BF16),
            pltpu.VMEM((2, EDGE, width), BF16),
            pltpu.VMEM((2, total, units), BF16),
            pltpu.VMEM((2, EDGE, units), BF16),
            pltpu.VMEM((width, 2 * rows), BF16),
            pltpu.VMEM((2 * depth, 2 * rows), BF16),
            pltpu.VMEM((2, total, units), F32),
            pltpu.VMEM((2, rows + 16, 128), F32),
            pltpu.VMEM((2, rows + 16, 128), F32),
            pltpu.VMEM((rows, units), F32),
            pltpu.VMEM((rows, units), BF16),
            pltpu.VMEM((CHUNKS, 2 * rows, cw), BF16),
            pltpu.VMEM((CHUNKS, 2 * rows, cw), BF16),
            pltpu.VMEM((rows, width), F32),
            pltpu.VMEM((rows, width), F32),
            pltpu.VMEM((CHUNKS, depth, cw), F32),
            pltpu.VMEM((CHUNKS, depth, cw), BF16),
            pltpu.VMEM((CHUNKS, depth, cw), BF16),
            pltpu.VMEM((CHUNKS, stacked_rows, cw), BF16),
            pltpu.VMEM((CHUNKS, stacked_rows, cw), BF16),
            pltpu.VMEM((CHUNKS, depth, cw), BF16),
            pltpu.VMEM((4, 24, units // 2), F32),
            pltpu.VMEM((bits + 2, 24, units // 2), F32),
            pltpu.VMEM((2, 24, units // 2), F32),
            dma((5 + CHUNKS,)),
            dma((5 * CHUNKS,)), dma((5 * CHUNKS,)),
            dma((5,)), dma((5,)),
            dma((CHUNKS, 2 + 2 * copies)), dma((CHUNKS, 2 + 2 * copies)),
            dma((bits + 3,)), dma((bits + 3,)),
        ],
        compiler_params=pltpu.CompilerParams(
            collective_id=0, has_side_effects=True, vmem_limit_bytes=60 * 1024 * 1024
        ),
        cost_estimate=pl.CostEstimate(
            flops=12 * rows * width * units, bytes_accessed=8 * rows * width, transcendentals=4 * rows * units
        ),
    )(
        window,
        token_codes.reshape(1, rows),
        embedding,
        weight,
        kernel,
        upstream,
    )
    block_result, grad_hidden, grad_weight, kernel_sum, table = pl.pallas_call(
        functools.partial(finish, factor),
        out_shape=(
            jax.ShapeDtypeStruct((rows, units), BF16),
            jax.ShapeDtypeStruct((rows, width), BF16),
            jax.ShapeDtypeStruct((depth, units), F32),
            jax.ShapeDtypeStruct((taps, units), F32),
            jax.ShapeDtypeStruct((vocab, width), F32),
        ),
        in_specs=[pl.BlockSpec(memory_space=pltpu.HBM)] * 5,
        out_specs=(pl.BlockSpec(memory_space=pltpu.HBM),) * 5,
        scratch_shapes=[
            pltpu.VMEM((rows, units), BF16),
            pltpu.VMEM((rows, width), BF16),
            pltpu.VMEM((taps, units), F32),
            pltpu.VMEM((vocab, width), F32),
            pltpu.VMEM((depth, units), BF16),
            pltpu.VMEM((depth, units), F32),
            dma((16,)),
        ],
        compiler_params=pltpu.CompilerParams(vmem_limit_bytes=60 * 1024 * 1024),
    )(block_result, grad_hidden, grad_weight, kernel_sum, table)
    return (
        block_result[None],
        grad_hidden[None],
        grad_weight,
        kernel_sum,
        table,
    )


def solution(mesh):
    in_specs = (P("dp", "seq", None), P("dp", "seq"), P(), P("dp", None), P(), P("dp", "seq", None))
    out_specs = (P("dp", "seq", None), P("dp", "seq", None), P("dp", None), P(), P())
    return jax.shard_map(
        functools.partial(local, mesh.shape["seq"]),
        mesh=mesh, in_specs=in_specs, out_specs=out_specs, check_vma=False,
    )
```
